512 devices in a mesh: tile: 64 (over y_hi, z, core), kern: 8 (over x, y_lo).
Axes of the slice: x: 4, y: 8 (y_hi: 4, y_lo: 2; y = y_hi * 2 + y_lo), z: 8, core: 2. Of those that a mesh axis runs over, the one named last changes fastest.
Arguments:
- levels: int32 [4096, 256], P('tile'), may hold values from 0 to 3
- jitter: float32 [4096, 256], P('tile'), may hold values from -6 to 6
- target: int32 [4096, 256], P('tile'), may hold values 0 or 1
- kernels: bfloat16 [24, 2, 35, 35], P('kern'), may hold values from -0.03125 to 0.03125
- kernel_weight: float32 [24], P('kern'), may hold values from 0.3 to 1
Outputs:
- mask_grad: float32 [4096, 256], P('tile', 'kern')
The draws below stay inside these ranges and needn't reach their ends.
All inputs are finite; a program needn't handle non-finite values. No bound on the sum of `target` on one device may be relied on, other than what follows from the above.
Results may differ from the reference program's by a relative error of at most 0.003.
Values may be sent and summed in bfloat16 or wider, within the bound.
No kernel may reach another device: no remote copies, remote signals or barrier semaphores. Data moves between devices by JAX's collectives and lax.ppermute only.
A program may use at most 128 MiB of HBM per device.

```python
import math
import jax
import jax.numpy as jnp
from jax import lax

WIDTH = 256
TAPS = 35
KERNELS = 24
NX = 4096


def set_ends(values, rng, least, largest):
    longest = values.shape.index(max(values.shape))
    spots = []
    for shift in (0, 1):
        where = [jax.random.randint(jax.random.fold_in(rng, axis), (), 0, length) for axis, length in enumerate(values.shape)]
        where[longest] = (where[longest] + shift) % values.shape[longest]
        spots.append(tuple(where))
    return values.at[spots[0]].set(least).at[spots[1]].set(largest)


def steps_of(rng, extent, cuts, least, largest):
    gain = 1.0
    for axis_at, blocks in cuts:
        steps = jax.random.uniform(jax.random.fold_in(jax.random.fold_in(rng, 6), axis_at), (blocks,), jnp.float32, least / len(cuts), largest / len(cuts))
        gain = gain * jnp.repeat(jnp.exp(steps), extent[axis_at] // blocks).reshape((-1,) + (1,) * (len(extent) - 1 - axis_at))
    return gain


def noise(stream_key, dims, deviation, bound, split=(), held_as=jnp.bfloat16):
    loudness = steps_of(stream_key, dims, split, -0.22, 0.18) if split else 1.0
    result = jax.random.normal(stream_key, dims, jnp.float32) * deviation * loudness
    return jnp.minimum(jnp.maximum(result, -bound), bound).astype(held_as)


def setup_inputs(seed: int = 0) -> dict:
    streams_of = jax.random.split(jax.random.key(seed), 6)
    levels = set_ends(jax.random.randint(streams_of[0], (NX, WIDTH), 0, 4), jax.random.fold_in(streams_of[0], 1), 0, 3).astype(jnp.int32)
    jitter = noise(streams_of[1], (NX, WIDTH), 1.0, 6.0, ((0, 64),), jnp.float32)
    target = set_ends((jax.random.randint(streams_of[2], (NX, WIDTH), 0, 2) < 1).astype(jnp.int32), jax.random.fold_in(streams_of[2], 1), 0, 1)
    kernels = noise(streams_of[3], (KERNELS, 2, TAPS, TAPS), (TAPS * TAPS * KERNELS) ** -0.5, 0.03125, ((0, 8),))
    kernel_weight = jnp.clip(jnp.exp(math.log(1.0) - 1.2039728 * jax.random.uniform(streams_of[4], (KERNELS,), jnp.float32) ** steps_of(streams_of[4], (KERNELS,), ((0, 8),), -0.2, 0.2)), 0.3, 1.0)
    return dict(levels=levels, jitter=jitter, target=target, kernels=kernels, kernel_weight=kernel_weight)


steepness = 10.0
threshold = 0.4


def reference(levels, jitter, target, kernels, kernel_weight):
    half_taps = TAPS // 2
    mask_field = jax.nn.sigmoid(levels.astype(jnp.float32) - 1.5 + jitter).astype(jnp.bfloat16)
    filters = kernels.astype(jnp.float32).reshape(KERNELS * 2, 1, TAPS, TAPS)
    fields = lax.conv_general_dilated(mask_field.astype(jnp.float32)[None, None], filters, (1, 1),
                                      ((half_taps, half_taps), (half_taps, half_taps)),
                                      precision=lax.Precision.HIGHEST)[0]
    weights = jnp.repeat(kernel_weight, 2)
    intensity = jnp.sum(weights[:, None, None] * fields * fields, axis=0)
    resist = jax.nn.sigmoid(steepness * (intensity - threshold))
    drive_field = 2.0 * (resist - target.astype(jnp.float32)) * steepness * resist * (1.0 - resist)
    adjoint = ((2.0 * weights)[:, None, None] * drive_field * fields).astype(jnp.bfloat16)
    flipped = kernels.astype(jnp.float32)[:, :, ::-1, ::-1].reshape(1, KERNELS * 2, TAPS, TAPS)
    mask_grad = lax.conv_general_dilated(adjoint.astype(jnp.float32)[None], flipped, (1, 1),
                                         ((half_taps, half_taps), (half_taps, half_taps)),
                                         precision=lax.Precision.HIGHEST)[0, 0]
    return mask_grad
```

```python
import functools

import jax
import jax.numpy as jnp
from jax import lax
from jax.experimental import pallas as pl
from jax.experimental.pallas import tpu as pltpu
from jax.sharding import PartitionSpec as P

steepness = 10.0
threshold = 0.4

TAPS = 35
HALF = 17
PITCH = 48
FLAT = 1792
TAP_LANES = TAPS * PITCH
GROUP = 8
FIELD_BLOCKS = 9
OUT_BLOCKS = 4
PARTNERS = 8
LOCAL = 6
CHANNELS = PARTNERS * LOCAL
ROWS = 64
OWN_COLS = 32
WIDTH = 256
FIELD_ROWS = GROUP * CHANNELS
TAP_PITCH = 40
VMEM = 50 * 1024 * 1024


def prepare(levels_ref, jitter_ref, target_ref, kernels_ref, weight_ref,
            mask_ref, goal_ref, next_ref, prev_ref, taps_ref):
    kern = lax.axis_index("kern")
    first_col = kern * OWN_COLS

    def columns(whole, before):
        shift = lax.rem(WIDTH + before - first_col, WIDTH)
        rolled = pltpu.roll(whole, shift, 1)[:, :128]
        col = lax.broadcasted_iota(jnp.int32, (ROWS, 128), 1) + (first_col - before)
        return jnp.where((col >= 0) & (col < WIDTH), rolled, 0.0)

    logits = levels_ref[...].astype(jnp.float32) - 1.5 + jitter_ref[...]
    mask = (1.0 / (1.0 + jnp.exp(-logits))).astype(jnp.bfloat16).astype(jnp.float32)
    mask = columns(mask, 2 * HALF)
    goal = columns(target_ref[...].astype(jnp.float32), HALF)
    mask_ref[...] = mask
    goal_ref[...] = goal
    next_ref[...] = jnp.concatenate([mask[24:64], goal[40:64]], 0).astype(jnp.bfloat16)
    prev_ref[...] = jnp.concatenate([mask[0:40], goal[0:24]], 0).astype(jnp.bfloat16)

    taps = kernels_ref[...].astype(jnp.float32)
    gap = jnp.zeros((LOCAL, PITCH - TAPS), jnp.float32)
    pieces = []
    for i in range(TAPS):
        pieces += [taps[:, i, :], gap]
    row = lax.broadcasted_iota(jnp.int32, (LOCAL, 1), 0)
    weight = jnp.where(row < 2, weight_ref[0], jnp.where(row < 4, weight_ref[1], weight_ref[2]))
    high = weight.astype(jnp.bfloat16).astype(jnp.float32)
    middle = (weight - high).astype(jnp.bfloat16).astype(jnp.float32)
    low = weight - high - middle
    lane = lax.broadcasted_iota(jnp.int32, (LOCAL, FLAT - TAP_LANES), 1)
    tail = jnp.where(lane == 0, high, jnp.where(lane == 1, middle, jnp.where(lane == 2, low, 0.0)))
    flat = jnp.concatenate(pieces + [tail], 1).astype(jnp.bfloat16)
    for partner in range(PARTNERS):
        taps_ref[partner] = flat


def gradient(mask_ref, goal_ref, up_ref, down_ref, taps_ref, out_ref,
             flat_ref, turned_ref, band_ref, image_ref, adjoint_ref, back_ref):
    tile = lax.axis_index("tile")
    kern = lax.axis_index("kern")
    tiles = lax.axis_size("tile")
    up = up_ref[...].astype(jnp.float32)
    down = down_ref[...].astype(jnp.float32)

    line = lax.broadcasted_iota(jnp.int32, (16, 128), 0) + 88
    mask = mask_ref[...]

    def circle(first_up):
        mixed = jnp.where(line >= first_up, up[0:16], down[24:40])
        return jnp.concatenate([mask, down[0:24], mixed, up[16:40]], 0).T

    image_above = circle(94)
    image_below = circle(98)
    goal = jnp.concatenate(
        [goal_ref[...], down[40:64], jnp.zeros((16, 128), jnp.float32), up[40:64]], 0
    ).T

    for i in range(TAPS):
        source = image_above if i < HALF else image_below
        turned = pltpu.roll(source, (HALF - i) % 128, 1)
        even = turned[0:112].astype(jnp.bfloat16)
        odd = turned[8:104].astype(jnp.bfloat16)
        for b in range(FIELD_BLOCKS):
            piece = even[8 * b : 8 * b + PITCH] if b % 2 == 0 else odd[8 * b - 8 : 8 * b - 8 + PITCH]
            image_ref[PITCH * i : PITCH * (i + 1), 128 * b : 128 * (b + 1)] = piece
    image_ref[TAP_LANES:, :] = jnp.zeros((FLAT - TAP_LANES, 128 * FIELD_BLOCKS), jnp.bfloat16)

    for partner in range(PARTNERS):
        flat_ref[LOCAL * partner : LOCAL * (partner + 1), :] = taps_ref[partner].astype(jnp.float32)
    last = flat_ref[:, TAP_LANES : TAP_LANES + 3]
    weight = last[:, 0:1] + last[:, 1:2] + last[:, 2:3]
    lane = lax.broadcasted_iota(jnp.int32, (CHANNELS, FLAT), 1)
    flat = jnp.where(lane < TAP_LANES, flat_ref[...], 0.0)
    for d in range(GROUP):
        shifted = flat if d == 0 else pltpu.roll(flat, d, 1)
        band_ref[CHANNELS * d : CHANNELS * (d + 1), :] = shifted.astype(jnp.bfloat16)

    turned_ref[...] = jnp.concatenate([flat, jnp.zeros((128 - CHANNELS, FLAT), jnp.float32)], 0).T
    pieces = []
    for j in range(TAPS):
        pieces.append(turned_ref[pl.ds(TAPS - 1 - j, TAPS, stride=PITCH), :][:, :CHANNELS])
    pieces.append(jnp.zeros((TAPS, CHANNELS * (PITCH - TAPS)), jnp.float32))
    backward = jnp.concatenate(pieces, 1)
    backward = jnp.concatenate(
        [backward, jnp.zeros((TAP_PITCH - TAPS, CHANNELS * PITCH), jnp.float32)], 0
    )
    for d in range(GROUP):
        shifted = backward if d == 0 else pltpu.roll(backward, CHANNELS * d, 1)
        back_ref[TAP_PITCH * d : TAP_PITCH * (d + 1), :] = shifted.astype(jnp.bfloat16)

    at = lax.broadcasted_iota(jnp.int32, (GROUP, 128), 1)
    at = jnp.where(at < 96, at, at - 128)
    row_in_clip = at + tile * ROWS
    row_ok = (row_in_clip >= 0) & (row_in_clip < tiles * ROWS)
    step = lax.broadcasted_iota(jnp.int32, (GROUP, 128), 0)
    for b in range(FIELD_BLOCKS):
        fields = jnp.dot(
            band_ref[...], image_ref[:, 128 * b : 128 * (b + 1)], preferred_element_type=jnp.float32
        )
        fields = fields.reshape(GROUP, CHANNELS, 128)
        weighted = fields * weight[None]
        intensity = jnp.sum(weighted * fields, axis=1)
        resist = 1.0 / (1.0 + jnp.exp(-steepness * (intensity - threshold)))
        drive = 2.0 * (resist - goal[8 * b : 8 * b + 8]) * steepness * resist * (1.0 - resist)
        col = step + (8 * b - HALF + kern * OWN_COLS)
        drive = jnp.where(row_ok & (col >= 0) & (col < WIDTH), drive, 0.0)
        adjoint = (2.0 * weighted * drive[:, None, :]).astype(jnp.bfloat16).reshape(FIELD_ROWS, 128)
        if b < FIELD_BLOCKS - 1:
            adjoint_ref[FIELD_ROWS * b : FIELD_ROWS * (b + 1), 0:128] = adjoint
        if b > 0:
            adjoint_ref[FIELD_ROWS * (b - 1) : FIELD_ROWS * b, 128:256] = adjoint

    grads = []
    for n in range(OUT_BLOCKS // 2):
        spread = jnp.dot(
            back_ref[...],
            adjoint_ref[2 * FIELD_ROWS * n : 2 * FIELD_ROWS * n + CHANNELS * PITCH, :],
            preferred_element_type=jnp.float32,
        )
        for half in range(2):
            for d in range(GROUP):
                part = spread[TAP_PITCH * d : TAP_PITCH * (d + 1), 128 * half : 128 * (half + 1)]
                part = pltpu.roll(part, 0, 1, stride=1, stride_axis=0)
                grads.append(jnp.sum(part, axis=0, keepdims=True))
    grad = pltpu.roll(jnp.concatenate(grads, 0), 128 - HALF, 1)
    grad = jnp.concatenate([grad, jnp.zeros((128 - OWN_COLS, 128), jnp.float32)], 0).T
    out_ref[...] = grad[:ROWS, :OWN_COLS]


def on_device(levels, jitter, target, kernels, kernel_weight):
    vmem = pl.BlockSpec(memory_space=pltpu.VMEM)
    smem = pl.BlockSpec(memory_space=pltpu.SMEM)
    f32, bf16 = jnp.float32, jnp.bfloat16
    mask, goal, to_next, to_prev, taps = pl.pallas_call(
        prepare,
        out_shape=(
            jax.ShapeDtypeStruct((ROWS, 128), f32),
            jax.ShapeDtypeStruct((ROWS, 128), f32),
            jax.ShapeDtypeStruct((ROWS, 128), bf16),
            jax.ShapeDtypeStruct((ROWS, 128), bf16),
            jax.ShapeDtypeStruct((PARTNERS, LOCAL, FLAT), bf16),
        ),
        in_specs=[vmem, vmem, vmem, vmem, smem],
        out_specs=(vmem,) * 5,
        compiler_params=pltpu.CompilerParams(vmem_limit_bytes=VMEM),
        name="prepare",
    )(levels, jitter, target, kernels.reshape(LOCAL, TAPS, TAPS), kernel_weight)
    ends = lax.axis_size("tile") - 1
    all_taps = lax.all_to_all(taps, "kern", 0, 0)
    up = lax.ppermute(to_next, "tile", [(i, i + 1) for i in range(ends)])
    down = lax.ppermute(to_prev, "tile", [(i + 1, i) for i in range(ends)])
    return pl.pallas_call(
        gradient,
        out_shape=jax.ShapeDtypeStruct((ROWS, OWN_COLS), f32),
        in_specs=[vmem] * 5,
        out_specs=vmem,
        scratch_shapes=[
            pltpu.VMEM((CHANNELS, FLAT), f32),
            pltpu.VMEM((FLAT, 128), f32),
            pltpu.VMEM((FIELD_ROWS, FLAT), bf16),
            pltpu.VMEM((FLAT, 128 * FIELD_BLOCKS), bf16),
            pltpu.VMEM((FIELD_ROWS * (FIELD_BLOCKS - 1), 256), bf16),
            pltpu.VMEM((GROUP * TAP_PITCH, CHANNELS * PITCH), bf16),
        ],
        compiler_params=pltpu.CompilerParams(vmem_limit_bytes=VMEM),
        name="gradient",
    )(mask, goal, up, down, all_taps)


def solution(mesh):
    return jax.shard_map(
        on_device,
        mesh=mesh,
        in_specs=(
            P("tile", None),
            P("tile", None),
            P("tile", None),
            P("kern", None, None, None),
            P("kern"),
        ),
        out_specs=P("tile", "kern"),
        check_vma=False,
    )
```

```python
import functools

import jax
import jax.numpy as jnp
from jax import lax
from jax.experimental import pallas as pl
from jax.experimental.pallas import tpu as pltpu
from jax.sharding import PartitionSpec as P

steepness = 10.0
threshold = 0.4

TAPS = 35
HALF = 17
PITCH = 48
FLAT = 1792
TAP_LANES = TAPS * PITCH
GROUP = 8
FIELD_BLOCKS = 9
OUT_BLOCKS = 4
PARTNERS = 8
LOCAL = 6
CHANNELS = PARTNERS * LOCAL
ROWS = 64
OWN_COLS = 32
WIDTH = 256
FIELD_ROWS = GROUP * CHANNELS
TAP_PITCH = 40
VMEM = 50 * 1024 * 1024


def prepare(levels_hbm, jitter_hbm, target_hbm, kernels_hbm, weight_hbm,
            mask_ref, goal_ref, next_ref, prev_ref, taps_ref,
            levels_ref, jitter_ref, target_ref, kernels_ref, weight_ref, arrived):
    copies = [
        pltpu.make_async_copy(source, place, arrived.at[n])
        for n, (source, place) in enumerate([
            (levels_hbm, levels_ref),
            (jitter_hbm, jitter_ref),
            (target_hbm, target_ref),
            (kernels_hbm, kernels_ref),
            (weight_hbm, weight_ref),
        ])
    ]
    for copy in copies:
        copy.start()
    kern = lax.axis_index("kern")
    first_col = kern * OWN_COLS

    def columns(whole, before):
        shift = lax.rem(WIDTH + before - first_col, WIDTH)
        rolled = pltpu.roll(whole, shift, 1)[:, :128]
        col = lax.broadcasted_iota(jnp.int32, (ROWS, 128), 1) + (first_col - before)
        return jnp.where((col >= 0) & (col < WIDTH), rolled, 0.0)

    for copy in copies:
        copy.wait()
    logits = levels_ref[...].astype(jnp.float32) - 1.5 + jitter_ref[...]
    mask = (1.0 / (1.0 + jnp.exp(-logits))).astype(jnp.bfloat16).astype(jnp.float32)
    mask = columns(mask, 2 * HALF)
    goal = columns(target_ref[...].astype(jnp.float32), HALF)
    mask_ref[...] = mask
    goal_ref[...] = goal
    next_ref[...] = jnp.concatenate([mask[24:64], goal[40:64]], 0).astype(jnp.bfloat16)
    prev_ref[...] = jnp.concatenate([mask[0:40], goal[0:24]], 0).astype(jnp.bfloat16)

    taps = kernels_ref[...].astype(jnp.float32)
    gap = jnp.zeros((LOCAL, PITCH - TAPS), jnp.float32)
    pieces = []
    for i in range(TAPS):
        pieces += [jnp.concatenate([taps[k, i] for k in range(LOCAL // 2)], 0), gap]
    row = lax.broadcasted_iota(jnp.int32, (LOCAL, 1), 0)
    weight = jnp.where(row < 2, weight_ref[0], jnp.where(row < 4, weight_ref[1], weight_ref[2]))
    high = weight.astype(jnp.bfloat16).astype(jnp.float32)
    middle = (weight - high).astype(jnp.bfloat16).astype(jnp.float32)
    low = weight - high - middle
    lane = lax.broadcasted_iota(jnp.int32, (LOCAL, FLAT - TAP_LANES), 1)
    tail = jnp.where(lane == 0, high, jnp.where(lane == 1, middle, jnp.where(lane == 2, low, 0.0)))
    flat = jnp.concatenate(pieces + [tail], 1).astype(jnp.bfloat16)
    for partner in range(PARTNERS):
        taps_ref[partner] = flat


def gradient(mask_ref, goal_ref, up_ref, down_ref, taps_ref, out_hbm,
             flat_ref, turned_ref, band_ref, image_ref, adjoint_ref, back_ref, out_ref, sent):
    tile = lax.axis_index("tile")
    kern = lax.axis_index("kern")
    tiles = lax.axis_size("tile")
    up = up_ref[...].astype(jnp.float32)
    down = down_ref[...].astype(jnp.float32)

    line = lax.broadcasted_iota(jnp.int32, (16, 128), 0) + 88
    mask = mask_ref[...]

    def circle(first_up):
        mixed = jnp.where(line >= first_up, up[0:16], down[24:40])
        return jnp.concatenate([mask, down[0:24], mixed, up[16:40]], 0).T

    image_above = circle(94)
    image_below = circle(98)
    goal = jnp.concatenate(
        [goal_ref[...], down[40:64], jnp.zeros((16, 128), jnp.float32), up[40:64]], 0
    ).T

    for i in range(TAPS):
        source = image_above if i < HALF else image_below
        turned = pltpu.roll(source, (HALF - i) % 128, 1)
        even = turned[0:112].astype(jnp.bfloat16)
        odd = turned[8:104].astype(jnp.bfloat16)
        for b in range(FIELD_BLOCKS):
            piece = even[8 * b : 8 * b + PITCH] if b % 2 == 0 else odd[8 * b - 8 : 8 * b - 8 + PITCH]
            image_ref[PITCH * i : PITCH * (i + 1), 128 * b : 128 * (b + 1)] = piece
    image_ref[TAP_LANES:, :] = jnp.zeros((FLAT - TAP_LANES, 128 * FIELD_BLOCKS), jnp.bfloat16)

    for partner in range(PARTNERS):
        flat_ref[LOCAL * partner : LOCAL * (partner + 1), :] = taps_ref[partner].astype(jnp.float32)
    last = flat_ref[:, TAP_LANES : TAP_LANES + 3]
    weight = last[:, 0:1] + last[:, 1:2] + last[:, 2:3]
    lane = lax.broadcasted_iota(jnp.int32, (CHANNELS, FLAT), 1)
    flat = jnp.where(lane < TAP_LANES, flat_ref[...], 0.0)
    for d in range(GROUP):
        shifted = flat if d == 0 else pltpu.roll(flat, d, 1)
        band_ref[CHANNELS * d : CHANNELS * (d + 1), :] = shifted.astype(jnp.bfloat16)

    turned_ref[...] = jnp.concatenate([flat, jnp.zeros((128 - CHANNELS, FLAT), jnp.float32)], 0).T
    pieces = []
    for j in range(TAPS):
        pieces.append(turned_ref[pl.ds(TAPS - 1 - j, TAPS, stride=PITCH), :][:, :CHANNELS])
    pieces.append(jnp.zeros((TAPS, CHANNELS * (PITCH - TAPS)), jnp.float32))
    backward = jnp.concatenate(pieces, 1)
    backward = jnp.concatenate(
        [backward, jnp.zeros((TAP_PITCH - TAPS, CHANNELS * PITCH), jnp.float32)], 0
    )
    for d in range(GROUP):
        shifted = backward if d == 0 else pltpu.roll(backward, CHANNELS * d, 1)
        back_ref[TAP_PITCH * d : TAP_PITCH * (d + 1), :] = shifted.astype(jnp.bfloat16)

    at = lax.broadcasted_iota(jnp.int32, (GROUP, 128), 1)
    at = jnp.where(at < 96, at, at - 128)
    row_in_clip = at + tile * ROWS
    row_ok = (row_in_clip >= 0) & (row_in_clip < tiles * ROWS)
    step = lax.broadcasted_iota(jnp.int32, (GROUP, 128), 0)
    for first in range(0, FIELD_BLOCKS, 2):
        count = min(2, FIELD_BLOCKS - first)
        together = jnp.dot(
            band_ref[...], image_ref[:, 128 * first : 128 * (first + count)], preferred_element_type=jnp.float32
        )
        for b in range(first, first + count):
            fields = together[:, 128 * (b - first) : 128 * (b - first + 1)]
            fields = fields.reshape(GROUP, CHANNELS, 128)
            weighted = fields * weight[None]
            intensity = jnp.sum(weighted * fields, axis=1)
            resist = 1.0 / (1.0 + jnp.exp(-steepness * (intensity - threshold)))
            drive = 2.0 * (resist - goal[8 * b : 8 * b + 8]) * steepness * resist * (1.0 - resist)
            col = step + (8 * b - HALF + kern * OWN_COLS)
            drive = jnp.where(row_ok & (col >= 0) & (col < WIDTH), drive, 0.0)
            adjoint = (2.0 * weighted * drive[:, None, :]).astype(jnp.bfloat16).reshape(FIELD_ROWS, 128)
            if b < FIELD_BLOCKS - 1:
                adjoint_ref[FIELD_ROWS * b : FIELD_ROWS * (b + 1), 0:128] = adjoint
            if b > 0:
                adjoint_ref[FIELD_ROWS * (b - 1) : FIELD_ROWS * b, 128:256] = adjoint

    grads = []
    for n in range(OUT_BLOCKS // 2):
        spread = jnp.dot(
            back_ref[...],
            adjoint_ref[2 * FIELD_ROWS * n : 2 * FIELD_ROWS * n + CHANNELS * PITCH, :],
            preferred_element_type=jnp.float32,
        )
        for half in range(2):
            for d in range(GROUP):
                part = spread[TAP_PITCH * d : TAP_PITCH * (d + 1), 128 * half : 128 * (half + 1)]
                part = pltpu.roll(part, 0, 1, stride=1, stride_axis=0)
                grads.append(jnp.sum(part, axis=0, keepdims=True))
    out_ref[...] = pltpu.roll(jnp.concatenate(grads, 0), 128 - HALF, 1)[:, :ROWS]
    copy = pltpu.make_async_copy(out_ref, out_hbm, sent)
    copy.start()
    copy.wait()


def on_device(levels, jitter, target, kernels, kernel_weight):
    vmem = pl.BlockSpec(memory_space=pltpu.VMEM)
    hbm = pl.BlockSpec(memory_space=pltpu.HBM)
    f32, bf16 = jnp.float32, jnp.bfloat16
    mask, goal, to_next, to_prev, taps = pl.pallas_call(
        prepare,
        out_shape=(
            jax.ShapeDtypeStruct((ROWS, 128), f32),
            jax.ShapeDtypeStruct((ROWS, 128), f32),
            jax.ShapeDtypeStruct((ROWS, 128), bf16),
            jax.ShapeDtypeStruct((ROWS, 128), bf16),
            jax.ShapeDtypeStruct((PARTNERS, LOCAL, FLAT), bf16),
        ),
        in_specs=[hbm] * 5,
        out_specs=(vmem,) * 5,
        scratch_shapes=[
            pltpu.VMEM((ROWS, WIDTH), jnp.int32),
            pltpu.VMEM((ROWS, WIDTH), f32),
            pltpu.VMEM((ROWS, WIDTH), jnp.int32),
            pltpu.VMEM((LOCAL // 2, TAPS, 2, TAPS), bf16),
            pltpu.SMEM((LOCAL // 2,), f32),
            pltpu.SemaphoreType.DMA((5,)),
        ],
        compiler_params=pltpu.CompilerParams(vmem_limit_bytes=VMEM),
        name="prepare",
    )(*(
        pltpu.with_memory_space_constraint(x, pltpu.HBM)
        for x in (levels, jitter, target, kernels.transpose(0, 2, 1, 3), kernel_weight)
    ))
    ends = lax.axis_size("tile") - 1
    all_taps = lax.all_to_all(taps, "kern", 0, 0)
    up = lax.ppermute(to_next, "tile", [(i, i + 1) for i in range(ends)])
    down = lax.ppermute(to_prev, "tile", [(i + 1, i) for i in range(ends)])
    return pl.pallas_call(
        gradient,
        out_shape=jax.ShapeDtypeStruct((OWN_COLS, ROWS), f32),
        in_specs=[vmem] * 5,
        out_specs=hbm,
        scratch_shapes=[
            pltpu.VMEM((CHANNELS, FLAT), f32),
            pltpu.VMEM((FLAT, 128), f32),
            pltpu.VMEM((FIELD_ROWS, FLAT), bf16),
            pltpu.VMEM((FLAT, 128 * FIELD_BLOCKS), bf16),
            pltpu.VMEM((FIELD_ROWS * (FIELD_BLOCKS - 1), 256), bf16),
            pltpu.VMEM((GROUP * TAP_PITCH, CHANNELS * PITCH), bf16),
            pltpu.VMEM((OWN_COLS, ROWS), f32),
            pltpu.SemaphoreType.DMA,
        ],
        compiler_params=pltpu.CompilerParams(vmem_limit_bytes=VMEM),
        name="gradient",
    )(mask, goal, up, down, all_taps).T


def solution(mesh):
    return jax.shard_map(
        on_device,
        mesh=mesh,
        in_specs=(
            P("tile", None),
            P("tile", None),
            P("tile", None),
            P("kern", None, None, None),
            P("kern"),
        ),
        out_specs=P("tile", "kern"),
        check_vma=False,
    )
```

```python
import functools

import jax
import jax.numpy as jnp
from jax import lax
from jax.experimental import pallas as pl
from jax.experimental.pallas import tpu as pltpu
from jax.sharding import PartitionSpec as P

steepness = 10.0
threshold = 0.4

TAPS = 35
HALF = 17
PITCH = 48
FLAT = 1792
TAP_LANES = TAPS * PITCH
GROUP = 8
FIELD_BLOCKS = 9
OUT_BLOCKS = 4
PARTNERS = 8
LOCAL = 6
CHANNELS = PARTNERS * LOCAL
ROWS = 64
SHARE = 8
HALF_FLAT = FLAT // 2
OWN_COLS = 32
WIDTH = 256
FIELD_ROWS = GROUP * CHANNELS
TAP_PITCH = 40
VMEM = 50 * 1024 * 1024


def prepare(levels_hbm, jitter_hbm, target_hbm, kernels_hbm, weight_hbm,
            mask_ref, goal_ref, far_ref, message_ref,
            levels_ref, jitter_ref, target_ref, kernels_ref, weight_ref, near_ref, arrived):
    copies = [
        pltpu.make_async_copy(source, place, arrived.at[n])
        for n, (source, place) in enumerate([
            (levels_hbm, levels_ref),
            (jitter_hbm, jitter_ref),
            (target_hbm, target_ref),
            (kernels_hbm, kernels_ref),
            (weight_hbm, weight_ref),
        ])
    ]
    for copy in copies:
        copy.start()
    kern = lax.axis_index("kern")
    core = lax.axis_index("core")
    first_col = kern * OWN_COLS

    def columns(whole, before):
        shift = lax.rem(WIDTH + before - first_col, WIDTH)
        rolled = pltpu.roll(whole, shift, 1)[:, :128]
        col = lax.broadcasted_iota(jnp.int32, (ROWS, 128), 1) + (first_col - before)
        return jnp.where((col >= 0) & (col < WIDTH), rolled, 0.0)

    for copy in copies:
        copy.wait()
    logits = levels_ref[...].astype(jnp.float32) - 1.5 + jitter_ref[...]
    mask = (1.0 / (1.0 + jnp.exp(-logits))).astype(jnp.bfloat16).astype(jnp.float32)
    goal = target_ref[...].astype(jnp.float32)
    own_mask = columns(mask, 2 * HALF)
    own_goal = columns(goal, HALF)
    mask_ref[...] = own_mask
    goal_ref[...] = own_goal
    odd = core == 1
    far_mask = jnp.where(odd, own_mask[24:64], own_mask[0:40])
    far_goal = jnp.where(odd, own_goal[40:64], own_goal[0:24])
    far_ref[...] = jnp.concatenate([far_mask, far_goal], 0).astype(jnp.bfloat16)
    near_ref[0:40] = jnp.where(odd, mask[0:40], mask[24:64])
    near_goal = jnp.where(odd, goal[0:24], goal[40:64])
    near_ref[40:64] = pltpu.roll(near_goal, WIDTH - HALF, 1)
    share = near_ref[pl.ds(pl.multiple_of(kern * SHARE, SHARE), SHARE), :]
    lane = lax.broadcasted_iota(jnp.int32, (SHARE, 128), 1)
    shares = []
    for partner in range(PARTNERS):
        start = partner * OWN_COLS - 2 * HALF
        rolled = pltpu.roll(share, (-start) % WIDTH, 1)[:, :128]
        inside = (lane >= -start) & (lane < WIDTH - start)
        shares.append(jnp.where(inside | (kern >= 40 // SHARE), rolled, 0.0).astype(jnp.bfloat16))

    taps = kernels_ref[...].astype(jnp.float32)
    gap = jnp.zeros((LOCAL, PITCH - TAPS), jnp.float32)
    pieces = []
    for i in range(TAPS):
        pieces += [jnp.concatenate([taps[k, i] for k in range(LOCAL // 2)], 0), gap]
    row = lax.broadcasted_iota(jnp.int32, (LOCAL, 1), 0)
    weight = jnp.where(row < 2, weight_ref[0], jnp.where(row < 4, weight_ref[1], weight_ref[2]))
    high = weight.astype(jnp.bfloat16).astype(jnp.float32)
    middle = (weight - high).astype(jnp.bfloat16).astype(jnp.float32)
    low = weight - high - middle
    lane = lax.broadcasted_iota(jnp.int32, (LOCAL, FLAT - TAP_LANES), 1)
    tail = jnp.where(lane == 0, high, jnp.where(lane == 1, middle, jnp.where(lane == 2, low, 0.0)))
    flat = jnp.concatenate(pieces + [tail], 1)
    part = jnp.where(odd, flat[:, HALF_FLAT:], flat[:, :HALF_FLAT])
    part = jnp.concatenate([part, jnp.zeros((SHARE - LOCAL, HALF_FLAT), jnp.float32)], 0).astype(jnp.bfloat16)
    for partner in range(PARTNERS):
        message = jnp.concatenate([part, shares[partner]], 1)
        for to_core in range(2):
            message_ref[PARTNERS * to_core + partner] = message


def gradient(mask_ref, goal_ref, far_ref, message_ref, out_hbm,
             flat_ref, turned_ref, band_ref, image_ref, adjoint_ref, back_ref, out_ref, sent):
    core = lax.axis_index("core")
    tile = lax.axis_index("pair") * 2 + core
    tiles = lax.axis_size("pair") * 2
    kern = lax.axis_index("kern")
    far = far_ref[...].astype(jnp.float32)
    near = jnp.concatenate(
        [message_ref[(1 - core) * PARTNERS + k, :, HALF_FLAT:].astype(jnp.float32) for k in range(PARTNERS)], 0
    )
    up = jnp.where(core == 1, near, far)
    down = jnp.where(core == 1, far, near)

    line = lax.broadcasted_iota(jnp.int32, (16, 128), 0) + 88
    mask = mask_ref[...]

    def circle(first_up):
        mixed = jnp.where(line >= first_up, up[0:16], down[24:40])
        return jnp.concatenate([mask, down[0:24], mixed, up[16:40]], 0).T

    image_above = circle(94)
    image_below = circle(98)
    goal = jnp.concatenate(
        [goal_ref[...], down[40:64], jnp.zeros((16, 128), jnp.float32), up[40:64]], 0
    ).T

    for i in range(TAPS):
        source = image_above if i < HALF else image_below
        turned = pltpu.roll(source, (HALF - i) % 128, 1)
        even = turned[0:112].astype(jnp.bfloat16)
        odd = turned[8:104].astype(jnp.bfloat16)
        for b in range(FIELD_BLOCKS):
            piece = even[8 * b : 8 * b + PITCH] if b % 2 == 0 else odd[8 * b - 8 : 8 * b - 8 + PITCH]
            image_ref[PITCH * i : PITCH * (i + 1), 128 * b : 128 * (b + 1)] = piece
    image_ref[TAP_LANES:, :] = jnp.zeros((FLAT - TAP_LANES, 128 * FIELD_BLOCKS), jnp.bfloat16)

    for partner in range(PARTNERS):
        for half in range(2):
            part = message_ref[PARTNERS * half + partner, :, :HALF_FLAT].astype(jnp.float32)
            flat_ref[LOCAL * partner : LOCAL * (partner + 1), HALF_FLAT * half : HALF_FLAT * (half + 1)] = part[:LOCAL]
    last = flat_ref[:, TAP_LANES : TAP_LANES + 3]
    weight = last[:, 0:1] + last[:, 1:2] + last[:, 2:3]
    lane = lax.broadcasted_iota(jnp.int32, (CHANNELS, FLAT), 1)
    flat = jnp.where(lane < TAP_LANES, flat_ref[...], 0.0)
    for d in range(GROUP):
        shifted = flat if d == 0 else pltpu.roll(flat, d, 1)
        band_ref[CHANNELS * d : CHANNELS * (d + 1), :] = shifted.astype(jnp.bfloat16)

    turned_ref[...] = jnp.concatenate([flat, jnp.zeros((128 - CHANNELS, FLAT), jnp.float32)], 0).T
    pieces = []
    for j in range(TAPS):
        pieces.append(turned_ref[pl.ds(TAPS - 1 - j, TAPS, stride=PITCH), :][:, :CHANNELS])
    pieces.append(jnp.zeros((TAPS, CHANNELS * (PITCH - TAPS)), jnp.float32))
    backward = jnp.concatenate(pieces, 1)
    backward = jnp.concatenate(
        [backward, jnp.zeros((TAP_PITCH - TAPS, CHANNELS * PITCH), jnp.float32)], 0
    )
    for d in range(GROUP):
        shifted = backward if d == 0 else pltpu.roll(backward, CHANNELS * d, 1)
        back_ref[TAP_PITCH * d : TAP_PITCH * (d + 1), :] = shifted.astype(jnp.bfloat16)

    at = lax.broadcasted_iota(jnp.int32, (GROUP, 128), 1)
    at = jnp.where(at < 96, at, at - 128)
    row_in_clip = at + tile * ROWS
    row_ok = (row_in_clip >= 0) & (row_in_clip < tiles * ROWS)
    step = lax.broadcasted_iota(jnp.int32, (GROUP, 128), 0)
    for first in range(0, FIELD_BLOCKS, 2):
        count = min(2, FIELD_BLOCKS - first)
        together = jnp.dot(
            band_ref[...], image_ref[:, 128 * first : 128 * (first + count)], preferred_element_type=jnp.float32
        )
        for b in range(first, first + count):
            fields = together[:, 128 * (b - first) : 128 * (b - first + 1)]
            fields = fields.reshape(GROUP, CHANNELS, 128)
            weighted = fields * weight[None]
            intensity = jnp.sum(weighted * fields, axis=1)
            resist = 1.0 / (1.0 + jnp.exp(-steepness * (intensity - threshold)))
            drive = 2.0 * (resist - goal[8 * b : 8 * b + 8]) * steepness * resist * (1.0 - resist)
            col = step + (8 * b - HALF + kern * OWN_COLS)
            drive = jnp.where(row_ok & (col >= 0) & (col < WIDTH), drive, 0.0)
            adjoint = (2.0 * weighted * drive[:, None, :]).astype(jnp.bfloat16).reshape(FIELD_ROWS, 128)
            if b < FIELD_BLOCKS - 1:
                adjoint_ref[FIELD_ROWS * b : FIELD_ROWS * (b + 1), 0:128] = adjoint
            if b > 0:
                adjoint_ref[FIELD_ROWS * (b - 1) : FIELD_ROWS * b, 128:256] = adjoint

    grads = []
    for n in range(OUT_BLOCKS // 2):
        spread = jnp.dot(
            back_ref[...],
            adjoint_ref[2 * FIELD_ROWS * n : 2 * FIELD_ROWS * n + CHANNELS * PITCH, :],
            preferred_element_type=jnp.float32,
        )
        for half in range(2):
            for d in range(GROUP):
                part = spread[TAP_PITCH * d : TAP_PITCH * (d + 1), 128 * half : 128 * (half + 1)]
                part = pltpu.roll(part, 0, 1, stride=1, stride_axis=0)
                grads.append(jnp.sum(part, axis=0, keepdims=True))
    out_ref[...] = pltpu.roll(jnp.concatenate(grads, 0), 128 - HALF, 1)[:, :ROWS]
    copy = pltpu.make_async_copy(out_ref, out_hbm, sent)
    copy.start()
    copy.wait()


def on_device(levels, jitter, target, kernels, kernel_weight):
    vmem = pl.BlockSpec(memory_space=pltpu.VMEM)
    hbm = pl.BlockSpec(memory_space=pltpu.HBM)
    f32, bf16 = jnp.float32, jnp.bfloat16
    mask, goal, to_far, message = pl.pallas_call(
        prepare,
        out_shape=(
            jax.ShapeDtypeStruct((ROWS, 128), f32),
            jax.ShapeDtypeStruct((ROWS, 128), f32),
            jax.ShapeDtypeStruct((ROWS, 128), bf16),
            jax.ShapeDtypeStruct((2 * PARTNERS, SHARE, HALF_FLAT + 128), bf16),
        ),
        in_specs=[hbm] * 5,
        out_specs=(vmem,) * 4,
        scratch_shapes=[
            pltpu.VMEM((ROWS, WIDTH), jnp.int32),
            pltpu.VMEM((ROWS, WIDTH), f32),
            pltpu.VMEM((ROWS, WIDTH), jnp.int32),
            pltpu.VMEM((LOCAL // 2, TAPS, 2, TAPS), bf16),
            pltpu.SMEM((LOCAL // 2,), f32),
            pltpu.VMEM((ROWS, WIDTH), f32),
            pltpu.SemaphoreType.DMA((5,)),
        ],
        compiler_params=pltpu.CompilerParams(vmem_limit_bytes=VMEM),
        name="prepare",
    )(*(
        pltpu.with_memory_space_constraint(x, pltpu.HBM)
        for x in (levels, jitter, target, kernels.transpose(0, 2, 1, 3), kernel_weight)
    ))
    pairs = lax.axis_size("pair")
    messages = lax.all_to_all(message, ("core", "kern"), 0, 0)
    meet = [(2 * p + 1, 2 * p + 2) for p in range(pairs - 1)]
    far = lax.ppermute(to_far, ("pair", "core"), meet + [(b, a) for a, b in meet])
    return pl.pallas_call(
        gradient,
        out_shape=jax.ShapeDtypeStruct((OWN_COLS, ROWS), f32),
        in_specs=[vmem] * 4,
        out_specs=hbm,
        scratch_shapes=[
            pltpu.VMEM((CHANNELS, FLAT), f32),
            pltpu.VMEM((FLAT, 128), f32),
            pltpu.VMEM((FIELD_ROWS, FLAT), bf16),
            pltpu.VMEM((FLAT, 128 * FIELD_BLOCKS), bf16),
            pltpu.VMEM((FIELD_ROWS * (FIELD_BLOCKS - 1), 256), bf16),
            pltpu.VMEM((GROUP * TAP_PITCH, CHANNELS * PITCH), bf16),
            pltpu.VMEM((OWN_COLS, ROWS), f32),
            pltpu.SemaphoreType.DMA,
        ],
        compiler_params=pltpu.CompilerParams(vmem_limit_bytes=VMEM),
        name="gradient",
    )(mask, goal, far, messages).T


def solution(mesh):
    tiles, partners = mesh.devices.shape
    mesh = jax.sharding.Mesh(mesh.devices.reshape(tiles // 2, 2, partners), ("pair", "core", "kern"))
    rows = P(("pair", "core"), None)
    return jax.shard_map(
        on_device,
        mesh=mesh,
        in_specs=(rows, rows, rows, P("kern", None, None, None), P("kern")),
        out_specs=P(("pair", "core"), "kern"),
        check_vma=False,
    )
```

```python
import functools

import jax
import jax.numpy as jnp
from jax import lax
from jax.experimental import pallas as pl
from jax.experimental.pallas import tpu as pltpu
from jax.sharding import PartitionSpec as P

steepness = 10.0
threshold = 0.4

TAPS = 35
HALF = 17
OWN_COLS = 32
PITCH = 48
FLAT = 1792
TAP_LANES = TAPS * PITCH
GROUP = 8
FIELD_BLOCKS = 9
FIELD_COLS = OWN_COLS + 2 * HALF
OUT_BLOCKS = 4
PARTNERS = 8
LOCAL = 6
CHANNELS = PARTNERS * LOCAL
ROWS = 64
SHARE = 8
HALF_FLAT = FLAT // 2
WIDTH = 256
FIELD_ROWS = GROUP * CHANNELS
TAP_PITCH = 40
DEPTH = 2048
VMEM = 50 * 1024 * 1024


def prepare(levels_hbm, jitter_hbm, target_hbm, kernels_hbm, weight_hbm,
            mask_ref, goal_ref, far_ref, message_ref,
            levels_ref, jitter_ref, target_ref, kernels_ref, weight_ref, near_ref, arrived):
    copies = [
        pltpu.make_async_copy(source, place, arrived.at[n])
        for n, (source, place) in enumerate([
            (levels_hbm, levels_ref),
            (jitter_hbm, jitter_ref),
            (target_hbm, target_ref),
            (kernels_hbm, kernels_ref),
            (weight_hbm, weight_ref),
        ])
    ]
    for copy in copies:
        copy.start()
    kern = lax.axis_index("kern")
    core = lax.axis_index("core")
    first_col = kern * OWN_COLS

    def columns(whole, before):
        shift = lax.rem(WIDTH + before - first_col, WIDTH)
        rolled = pltpu.roll(whole, shift, 1)[:, :128]
        col = lax.broadcasted_iota(jnp.int32, (ROWS, 128), 1) + (first_col - before)
        return jnp.where((col >= 0) & (col < WIDTH), rolled, 0.0)

    for copy in copies:
        copy.wait()
    logits = levels_ref[...].astype(jnp.float32) - 1.5 + jitter_ref[...]
    mask = (1.0 / (1.0 + jnp.exp(-logits))).astype(jnp.bfloat16).astype(jnp.float32)
    goal = target_ref[...].astype(jnp.float32)
    own_mask = columns(mask, 2 * HALF)
    own_goal = columns(goal, HALF)
    mask_ref[...] = own_mask
    goal_ref[...] = own_goal
    odd = core == 1
    far_mask = jnp.where(odd, own_mask[24:64], own_mask[0:40])
    far_goal = jnp.where(odd, own_goal[40:64], own_goal[0:24])
    far_ref[...] = jnp.concatenate([far_mask, far_goal], 0).astype(jnp.bfloat16)
    near_ref[0:40] = jnp.where(odd, mask[0:40], mask[24:64])
    near_goal = jnp.where(odd, goal[0:24], goal[40:64])
    near_ref[40:64] = pltpu.roll(near_goal, WIDTH - HALF, 1)
    share = near_ref[pl.ds(pl.multiple_of(kern * SHARE, SHARE), SHARE), :]
    lane = lax.broadcasted_iota(jnp.int32, (SHARE, 128), 1)
    shares = []
    for partner in range(PARTNERS):
        start = partner * OWN_COLS - 2 * HALF
        rolled = pltpu.roll(share, (-start) % WIDTH, 1)[:, :128]
        inside = (lane >= -start) & (lane < WIDTH - start)
        shares.append(jnp.where(inside | (kern >= 40 // SHARE), rolled, 0.0).astype(jnp.bfloat16))

    taps = kernels_ref[...].astype(jnp.float32)
    gap = jnp.zeros((LOCAL, PITCH - TAPS), jnp.float32)
    pieces = []
    for i in range(TAPS):
        pieces += [jnp.concatenate([taps[k, i] for k in range(LOCAL // 2)], 0), gap]
    row = lax.broadcasted_iota(jnp.int32, (LOCAL, 1), 0)
    weight = jnp.where(row < 2, weight_ref[0], jnp.where(row < 4, weight_ref[1], weight_ref[2]))
    high = weight.astype(jnp.bfloat16).astype(jnp.float32)
    middle = (weight - high).astype(jnp.bfloat16).astype(jnp.float32)
    low = weight - high - middle
    lane = lax.broadcasted_iota(jnp.int32, (LOCAL, FLAT - TAP_LANES), 1)
    tail = jnp.where(lane == 0, high, jnp.where(lane == 1, middle, jnp.where(lane == 2, low, 0.0)))
    flat = jnp.concatenate(pieces + [tail], 1)
    part = jnp.where(odd, flat[:, HALF_FLAT:], flat[:, :HALF_FLAT])
    part = jnp.concatenate([part, jnp.zeros((SHARE - LOCAL, HALF_FLAT), jnp.float32)], 0).astype(jnp.bfloat16)
    for partner in range(PARTNERS):
        message = jnp.concatenate([part, shares[partner]], 1)
        for to_core in range(2):
            message_ref[PARTNERS * to_core + partner] = message


def gradient(mask_ref, goal_ref, far_ref, message_ref, out_hbm,
             flat_ref, turned_ref, band_ref, even_ref, odd_ref, adjoint_ref, back_ref, out_ref, sent):
    core = lax.axis_index("core")
    tile = lax.axis_index("pair") * 2 + core
    tiles = lax.axis_size("pair") * 2
    kern = lax.axis_index("kern")
    far = far_ref[...].astype(jnp.float32)
    near = jnp.concatenate(
        [message_ref[(1 - core) * PARTNERS + k, :, HALF_FLAT:].astype(jnp.float32) for k in range(PARTNERS)], 0
    )
    up = jnp.where(core == 1, near, far)
    down = jnp.where(core == 1, far, near)

    line = lax.broadcasted_iota(jnp.int32, (16, 128), 0) + 88
    mask = mask_ref[...]

    def circle(first_up):
        mixed = jnp.where(line >= first_up, up[0:16], down[24:40])
        return jnp.concatenate([mask, down[0:24], mixed, up[16:40]], 0).T

    image_above = circle(94)
    image_below = circle(98)
    goal = jnp.concatenate(
        [goal_ref[...], down[40:64], jnp.zeros((16, 128), jnp.float32), up[40:64]], 0
    ).T

    for i in range(TAPS):
        source = image_above if i < HALF else image_below
        turned = pltpu.roll(source, (HALF - i) % 128, 1)
        even_ref[i] = turned[0:112].astype(jnp.bfloat16)
        odd_ref[i] = turned[8:104].astype(jnp.bfloat16)

    for partner in range(PARTNERS):
        for half in range(2):
            part = message_ref[PARTNERS * half + partner, :, :HALF_FLAT].astype(jnp.float32)
            flat_ref[LOCAL * partner : LOCAL * (partner + 1), HALF_FLAT * half : HALF_FLAT * (half + 1)] = part[:LOCAL]
    last = flat_ref[:, TAP_LANES : TAP_LANES + 3]
    weight = last[:, 0:1] + last[:, 1:2] + last[:, 2:3]
    lane = lax.broadcasted_iota(jnp.int32, (CHANNELS, FLAT), 1)
    flat = jnp.where(lane < TAP_LANES, flat_ref[...], 0.0)
    for d in range(GROUP):
        shifted = flat if d == 0 else pltpu.roll(flat, d, 1)
        band_ref[CHANNELS * d : CHANNELS * (d + 1), :] = shifted.astype(jnp.bfloat16)

    turned_ref[...] = jnp.concatenate([flat, jnp.zeros((128 - CHANNELS, FLAT), jnp.float32)], 0).T
    pieces = []
    for j in range(TAPS):
        pieces.append(turned_ref[pl.ds(TAPS - 1 - j, TAPS, stride=PITCH), :][:, :CHANNELS])
    pieces.append(jnp.zeros((TAPS, CHANNELS * (PITCH - TAPS)), jnp.float32))
    backward = jnp.concatenate(pieces, 1)
    backward = jnp.concatenate(
        [backward, jnp.zeros((TAP_PITCH - TAPS, CHANNELS * PITCH), jnp.float32)], 0
    )
    for d in range(GROUP):
        shifted = backward if d == 0 else pltpu.roll(backward, CHANNELS * d, 1)
        back_ref[TAP_PITCH * d : TAP_PITCH * (d + 1), :] = shifted.astype(jnp.bfloat16)

    at = lax.broadcasted_iota(jnp.int32, (GROUP, 128), 1)
    at = jnp.where(at < 96, at, at - 128)
    row_in_clip = at + tile * ROWS
    row_ok = (row_in_clip >= 0) & (row_in_clip < tiles * ROWS)
    step = lax.broadcasted_iota(jnp.int32, (GROUP, 128), 0)
    for first in range(0, FIELD_BLOCKS, 2):
        count = min(2, FIELD_BLOCKS - first)
        groups = min(GROUP, FIELD_COLS - GROUP * first)
        together = jnp.dot(
            band_ref[: CHANNELS * groups, :TAP_LANES],
            jnp.concatenate([
                (even_ref if b % 2 == 0 else odd_ref)[:, 16 * (b // 2) : 16 * (b // 2) + PITCH, :].reshape(TAP_LANES, 128)
                for b in range(first, first + count)
            ], 1),
            preferred_element_type=jnp.float32,
        )
        for b in range(first, first + count):
            fields = together[:, 128 * (b - first) : 128 * (b - first + 1)]
            fields = fields.reshape(groups, CHANNELS, 128)
            weighted = fields * weight[None]
            intensity = jnp.sum(weighted * fields, axis=1)
            resist = 1.0 / (1.0 + jnp.exp(-steepness * (intensity - threshold)))
            drive = 2.0 * (resist - goal[8 * b : 8 * b + groups]) * steepness * resist * (1.0 - resist)
            col = step[:groups] + (8 * b - HALF + kern * OWN_COLS)
            drive = jnp.where(row_ok[:groups] & (col >= 0) & (col < WIDTH), drive, 0.0)
            adjoint = (2.0 * weighted * drive[:, None, :]).astype(jnp.bfloat16).reshape(CHANNELS * groups, 128)
            if groups < GROUP:
                rest = jnp.zeros((FIELD_ROWS - CHANNELS * groups, 128), jnp.bfloat16)
                adjoint = jnp.concatenate([adjoint, rest], 0)
            if b < FIELD_BLOCKS - 1:
                adjoint_ref[FIELD_ROWS * b : FIELD_ROWS * (b + 1), 0:128] = adjoint
            if b > 0:
                adjoint_ref[FIELD_ROWS * (b - 1) : FIELD_ROWS * b, 128:256] = adjoint

    grads = []
    for n in range(OUT_BLOCKS // 2):
        spread = jnp.dot(
            back_ref[:, :DEPTH],
            adjoint_ref[2 * FIELD_ROWS * n : 2 * FIELD_ROWS * n + DEPTH, :],
            preferred_element_type=jnp.float32,
        )
        for half in range(2):
            for d in range(GROUP):
                part = spread[TAP_PITCH * d : TAP_PITCH * (d + 1), 128 * half : 128 * (half + 1)]
                part = pltpu.roll(part, 0, 1, stride=1, stride_axis=0)
                grads.append(jnp.sum(part, axis=0, keepdims=True))
    out_ref[...] = pltpu.roll(jnp.concatenate(grads, 0), 128 - HALF, 1)[:, :ROWS]
    copy = pltpu.make_async_copy(out_ref, out_hbm, sent)
    copy.start()
    copy.wait()


def on_device(levels, jitter, target, kernels, kernel_weight):
    vmem = pl.BlockSpec(memory_space=pltpu.VMEM)
    hbm = pl.BlockSpec(memory_space=pltpu.HBM)
    f32, bf16 = jnp.float32, jnp.bfloat16
    mask, goal, to_far, message = pl.pallas_call(
        prepare,
        out_shape=(
            jax.ShapeDtypeStruct((ROWS, 128), f32),
            jax.ShapeDtypeStruct((ROWS, 128), f32),
            jax.ShapeDtypeStruct((ROWS, 128), bf16),
            jax.ShapeDtypeStruct((2 * PARTNERS, SHARE, HALF_FLAT + 128), bf16),
        ),
        in_specs=[hbm] * 5,
        out_specs=(vmem,) * 4,
        scratch_shapes=[
            pltpu.VMEM((ROWS, WIDTH), jnp.int32),
            pltpu.VMEM((ROWS, WIDTH), f32),
            pltpu.VMEM((ROWS, WIDTH), jnp.int32),
            pltpu.VMEM((LOCAL // 2, TAPS, 2, TAPS), bf16),
            pltpu.SMEM((LOCAL // 2,), f32),
            pltpu.VMEM((ROWS, WIDTH), f32),
            pltpu.SemaphoreType.DMA((5,)),
        ],
        compiler_params=pltpu.CompilerParams(vmem_limit_bytes=VMEM),
        name="prepare",
    )(*(
        pltpu.with_memory_space_constraint(x, pltpu.HBM)
        for x in (levels, jitter, target, kernels.transpose(0, 2, 1, 3), kernel_weight)
    ))
    pairs = lax.axis_size("pair")
    messages = lax.all_to_all(message, ("core", "kern"), 0, 0)
    meet = [(2 * p + 1, 2 * p + 2) for p in range(pairs - 1)]
    far = lax.ppermute(to_far, ("pair", "core"), meet + [(b, a) for a, b in meet])
    return pl.pallas_call(
        gradient,
        out_shape=jax.ShapeDtypeStruct((OWN_COLS, ROWS), f32),
        in_specs=[vmem] * 4,
        out_specs=hbm,
        scratch_shapes=[
            pltpu.VMEM((CHANNELS, FLAT), f32),
            pltpu.VMEM((FLAT, 128), f32),
            pltpu.VMEM((FIELD_ROWS, FLAT), bf16),
            pltpu.VMEM((TAPS, 112, 128), bf16),
            pltpu.VMEM((TAPS, 96, 128), bf16),
            pltpu.VMEM((FIELD_ROWS * (FIELD_BLOCKS - 1), 256), bf16),
            pltpu.VMEM((GROUP * TAP_PITCH, CHANNELS * PITCH), bf16),
            pltpu.VMEM((OWN_COLS, ROWS), f32),
            pltpu.SemaphoreType.DMA,
        ],
        compiler_params=pltpu.CompilerParams(vmem_limit_bytes=VMEM),
        name="gradient",
    )(mask, goal, far, messages).T


def solution(mesh):
    tiles, partners = mesh.devices.shape
    mesh = jax.sharding.Mesh(mesh.devices.reshape(tiles // 2, 2, partners), ("pair", "core", "kern"))
    rows = P(("pair", "core"), None)
    return jax.shard_map(
        on_device,
        mesh=mesh,
        in_specs=(rows, rows, rows, P("kern", None, None, None), P("kern")),
        out_specs=P(("pair", "core"), "kern"),
        check_vma=False,
    )
```

```python
import functools

import jax
import jax.numpy as jnp
from jax import lax
from jax.experimental import pallas as pl
from jax.experimental.pallas import tpu as pltpu
from jax.sharding import PartitionSpec as P

steepness = 10.0
threshold = 0.4

TAPS = 35
HALF = 17
OWN_COLS = 32
PITCH = 48
FLAT = 1792
TAP_LANES = TAPS * PITCH
GROUP = 8
FIELD_BLOCKS = 9
FIELD_COLS = OWN_COLS + 2 * HALF
OUT_BLOCKS = 4
PARTNERS = 8
LOCAL = 6
CHANNELS = PARTNERS * LOCAL
ROWS = 64
RUN = 16
RELAYED = (32, 48)
LATE_COST = 33 * 10**8
SHARE = 8
HALF_FLAT = FLAT // 2
WIDTH = 256
FIELD_ROWS = GROUP * CHANNELS
TAP_PITCH = 40
DEPTH = 2048
VMEM = 50 * 1024 * 1024


def prepare(levels_hbm, jitter_hbm, target_hbm, kernels_hbm, weight_hbm,
            mask_ref, goal_ref, far_ref, message_ref,
            levels_ref, jitter_ref, target_ref, kernels_ref, weight_ref, near_ref, arrived):
    copies = [
        pltpu.make_async_copy(source, place, arrived.at[n])
        for n, (source, place) in enumerate([
            (levels_hbm, levels_ref),
            (jitter_hbm, jitter_ref),
            (target_hbm, target_ref),
            (kernels_hbm, kernels_ref),
            (weight_hbm, weight_ref),
        ])
    ]
    for copy in copies:
        copy.start()
    kern = lax.axis_index("kern")
    core = lax.axis_index("core")
    first_col = kern * OWN_COLS

    def columns(whole, before):
        shift = lax.rem(WIDTH + before - first_col, WIDTH)
        rolled = pltpu.roll(whole, shift, 1)[:, :128]
        col = lax.broadcasted_iota(jnp.int32, (ROWS, 128), 1) + (first_col - before)
        return jnp.where((col >= 0) & (col < WIDTH), rolled, 0.0)

    for copy in copies:
        copy.wait()
    logits = levels_ref[...].astype(jnp.float32) - 1.5 + jitter_ref[...]
    mask = (1.0 / (1.0 + jnp.exp(-logits))).astype(jnp.bfloat16).astype(jnp.float32)
    goal = target_ref[...].astype(jnp.float32)
    own_mask = columns(mask, 2 * HALF)
    own_goal = columns(goal, HALF)
    mask_ref[...] = own_mask
    goal_ref[...] = own_goal
    odd = core == 1
    far_mask = jnp.where(odd, own_mask[24:64], own_mask[0:40])
    far_goal = jnp.where(odd, own_goal[40:64], own_goal[0:24])
    far_ref[...] = jnp.concatenate([far_mask, far_goal], 0).astype(jnp.bfloat16)
    near_ref[0:40] = jnp.where(odd, mask[0:40], mask[24:64])
    near_goal = jnp.where(odd, goal[0:24], goal[40:64])
    near_ref[40:64] = pltpu.roll(near_goal, WIDTH - HALF, 1)
    share = near_ref[pl.ds(pl.multiple_of(kern * SHARE, SHARE), SHARE), :]
    lane = lax.broadcasted_iota(jnp.int32, (SHARE, 128), 1)
    shares = []
    for partner in range(PARTNERS):
        start = partner * OWN_COLS - 2 * HALF
        rolled = pltpu.roll(share, (-start) % WIDTH, 1)[:, :128]
        inside = (lane >= -start) & (lane < WIDTH - start)
        shares.append(jnp.where(inside | (kern >= 40 // SHARE), rolled, 0.0).astype(jnp.bfloat16))

    taps = kernels_ref[...].astype(jnp.float32)
    gap = jnp.zeros((LOCAL, PITCH - TAPS), jnp.float32)
    pieces = []
    for i in range(TAPS):
        pieces += [jnp.concatenate([taps[k, i] for k in range(LOCAL // 2)], 0), gap]
    row = lax.broadcasted_iota(jnp.int32, (LOCAL, 1), 0)
    weight = jnp.where(row < 2, weight_ref[0], jnp.where(row < 4, weight_ref[1], weight_ref[2]))
    high = weight.astype(jnp.bfloat16).astype(jnp.float32)
    middle = (weight - high).astype(jnp.bfloat16).astype(jnp.float32)
    low = weight - high - middle
    lane = lax.broadcasted_iota(jnp.int32, (LOCAL, FLAT - TAP_LANES), 1)
    tail = jnp.where(lane == 0, high, jnp.where(lane == 1, middle, jnp.where(lane == 2, low, 0.0)))
    flat = jnp.concatenate(pieces + [tail], 1)
    part = jnp.where(odd, flat[:, HALF_FLAT:], flat[:, :HALF_FLAT])
    part = jnp.concatenate([part, jnp.zeros((SHARE - LOCAL, HALF_FLAT), jnp.float32)], 0).astype(jnp.bfloat16)
    for partner in range(PARTNERS):
        message = jnp.concatenate([part, shares[partner]], 1)
        for to_core in range(2):
            message_ref[PARTNERS * to_core + partner] = message


def either(far_ref, late_ref, passed_ref, rows_ref):
    tile = lax.axis_index("pair") * 2 + lax.axis_index("core")
    far = far_ref[...].astype(jnp.float32)
    for start in RELAYED:
        far = jnp.where(tile == start + RUN - 1, 0.0, far)
    rows_ref[...] = far + late_ref[...].astype(jnp.float32) + passed_ref[...].astype(jnp.float32)


def gradient(mask_ref, goal_ref, far_ref, message_ref, out_hbm,
             flat_ref, turned_ref, band_ref, even_ref, odd_ref, adjoint_ref, back_ref, out_ref, sent):
    core = lax.axis_index("core")
    tile = lax.axis_index("pair") * 2 + core
    tiles = lax.axis_size("pair") * 2
    kern = lax.axis_index("kern")
    far = far_ref[...]
    near = jnp.concatenate(
        [message_ref[(1 - core) * PARTNERS + k, :, HALF_FLAT:].astype(jnp.float32) for k in range(PARTNERS)], 0
    )
    up = jnp.where(core == 1, near, far)
    down = jnp.where(core == 1, far, near)

    line = lax.broadcasted_iota(jnp.int32, (16, 128), 0) + 88
    mask = mask_ref[...]

    def circle(first_up):
        mixed = jnp.where(line >= first_up, up[0:16], down[24:40])
        return jnp.concatenate([mask, down[0:24], mixed, up[16:40]], 0).T

    image_above = circle(94)
    image_below = circle(98)
    goal = jnp.concatenate(
        [goal_ref[...], down[40:64], jnp.zeros((16, 128), jnp.float32), up[40:64]], 0
    ).T

    for i in range(TAPS):
        source = image_above if i < HALF else image_below
        turned = pltpu.roll(source, (HALF - i) % 128, 1)
        even_ref[i] = turned[0:112].astype(jnp.bfloat16)
        odd_ref[i] = turned[8:104].astype(jnp.bfloat16)

    for partner in range(PARTNERS):
        for half in range(2):
            part = message_ref[PARTNERS * half + partner, :, :HALF_FLAT].astype(jnp.float32)
            flat_ref[LOCAL * partner : LOCAL * (partner + 1), HALF_FLAT * half : HALF_FLAT * (half + 1)] = part[:LOCAL]
    last = flat_ref[:, TAP_LANES : TAP_LANES + 3]
    weight = last[:, 0:1] + last[:, 1:2] + last[:, 2:3]
    lane = lax.broadcasted_iota(jnp.int32, (CHANNELS, FLAT), 1)
    flat = jnp.where(lane < TAP_LANES, flat_ref[...], 0.0)
    for d in range(GROUP):
        shifted = flat if d == 0 else pltpu.roll(flat, d, 1)
        band_ref[CHANNELS * d : CHANNELS * (d + 1), :] = shifted.astype(jnp.bfloat16)

    turned_ref[...] = jnp.concatenate([flat, jnp.zeros((128 - CHANNELS, FLAT), jnp.float32)], 0).T
    pieces = []
    for j in range(TAPS):
        pieces.append(turned_ref[pl.ds(TAPS - 1 - j, TAPS, stride=PITCH), :][:, :CHANNELS])
    pieces.append(jnp.zeros((TAPS, CHANNELS * (PITCH - TAPS)), jnp.float32))
    backward = jnp.concatenate(pieces, 1)
    backward = jnp.concatenate(
        [backward, jnp.zeros((TAP_PITCH - TAPS, CHANNELS * PITCH), jnp.float32)], 0
    )
    for d in range(GROUP):
        shifted = backward if d == 0 else pltpu.roll(backward, CHANNELS * d, 1)
        back_ref[TAP_PITCH * d : TAP_PITCH * (d + 1), :] = shifted.astype(jnp.bfloat16)

    at = lax.broadcasted_iota(jnp.int32, (GROUP, 128), 1)
    at = jnp.where(at < 96, at, at - 128)
    row_in_clip = at + tile * ROWS
    row_ok = (row_in_clip >= 0) & (row_in_clip < tiles * ROWS)
    step = lax.broadcasted_iota(jnp.int32, (GROUP, 128), 0)
    for first in range(0, FIELD_BLOCKS, 2):
        count = min(2, FIELD_BLOCKS - first)
        groups = min(GROUP, FIELD_COLS - GROUP * first)
        together = jnp.dot(
            band_ref[: CHANNELS * groups, :TAP_LANES],
            jnp.concatenate([
                (even_ref if b % 2 == 0 else odd_ref)[:, 16 * (b // 2) : 16 * (b // 2) + PITCH, :].reshape(TAP_LANES, 128)
                for b in range(first, first + count)
            ], 1),
            preferred_element_type=jnp.float32,
        )
        for b in range(first, first + count):
            fields = together[:, 128 * (b - first) : 128 * (b - first + 1)]
            fields = fields.reshape(groups, CHANNELS, 128)
            weighted = fields * weight[None]
            intensity = jnp.sum(weighted * fields, axis=1)
            resist = 1.0 / (1.0 + jnp.exp(-steepness * (intensity - threshold)))
            drive = 2.0 * (resist - goal[8 * b : 8 * b + groups]) * steepness * resist * (1.0 - resist)
            col = step[:groups] + (8 * b - HALF + kern * OWN_COLS)
            drive = jnp.where(row_ok[:groups] & (col >= 0) & (col < WIDTH), drive, 0.0)
            adjoint = (2.0 * weighted * drive[:, None, :]).astype(jnp.bfloat16).reshape(CHANNELS * groups, 128)
            if groups < GROUP:
                rest = jnp.zeros((FIELD_ROWS - CHANNELS * groups, 128), jnp.bfloat16)
                adjoint = jnp.concatenate([adjoint, rest], 0)
            if b < FIELD_BLOCKS - 1:
                adjoint_ref[FIELD_ROWS * b : FIELD_ROWS * (b + 1), 0:128] = adjoint
            if b > 0:
                adjoint_ref[FIELD_ROWS * (b - 1) : FIELD_ROWS * b, 128:256] = adjoint

    grads = []
    for n in range(OUT_BLOCKS // 2):
        spread = jnp.dot(
            back_ref[:, :DEPTH],
            adjoint_ref[2 * FIELD_ROWS * n : 2 * FIELD_ROWS * n + DEPTH, :],
            preferred_element_type=jnp.float32,
        )
        for half in range(2):
            for d in range(GROUP):
                part = spread[TAP_PITCH * d : TAP_PITCH * (d + 1), 128 * half : 128 * (half + 1)]
                part = pltpu.roll(part, 0, 1, stride=1, stride_axis=0)
                grads.append(jnp.sum(part, axis=0, keepdims=True))
    out_ref[...] = pltpu.roll(jnp.concatenate(grads, 0), 128 - HALF, 1)[:, :ROWS]
    copy = pltpu.make_async_copy(out_ref, out_hbm, sent)
    copy.start()
    copy.wait()


def on_device(levels, jitter, target, kernels, kernel_weight):
    vmem = pl.BlockSpec(memory_space=pltpu.VMEM)
    hbm = pl.BlockSpec(memory_space=pltpu.HBM)
    f32, bf16 = jnp.float32, jnp.bfloat16
    mask, goal, to_far, message = pl.pallas_call(
        prepare,
        out_shape=(
            jax.ShapeDtypeStruct((ROWS, 128), f32),
            jax.ShapeDtypeStruct((ROWS, 128), f32),
            jax.ShapeDtypeStruct((ROWS, 128), bf16),
            jax.ShapeDtypeStruct((2 * PARTNERS, SHARE, HALF_FLAT + 128), bf16),
        ),
        in_specs=[hbm] * 5,
        out_specs=(vmem,) * 4,
        scratch_shapes=[
            pltpu.VMEM((ROWS, WIDTH), jnp.int32),
            pltpu.VMEM((ROWS, WIDTH), f32),
            pltpu.VMEM((ROWS, WIDTH), jnp.int32),
            pltpu.VMEM((LOCAL // 2, TAPS, 2, TAPS), bf16),
            pltpu.SMEM((LOCAL // 2,), f32),
            pltpu.VMEM((ROWS, WIDTH), f32),
            pltpu.SemaphoreType.DMA((5,)),
        ],
        compiler_params=pltpu.CompilerParams(vmem_limit_bytes=VMEM),
        name="prepare",
    )(*(
        pltpu.with_memory_space_constraint(x, pltpu.HBM)
        for x in (levels, jitter, target, kernels.transpose(0, 2, 1, 3), kernel_weight)
    ))
    tiles = lax.axis_size("pair") * 2
    axes = ("pair", "core")
    starts = range(RUN, tiles, RUN)
    late = lax.ppermute(to_far, axes, [(t - 1, t) for t in starts])
    messages = lax.all_to_all(message, ("core", "kern"), 0, 0)
    meet = [(t, t + 1) for t in range(1, tiles - 1, 2)]
    moves = [(a, b) for a, b in meet if b not in starts]
    moves += [(b, a) for a, b in meet if b not in RELAYED] + [(t, t + RUN - 1) for t in RELAYED]
    ends = lax.axis_index(axes) % RUN == RUN - 1
    far = lax.ppermute(jnp.where(ends, late, to_far), axes, moves)
    passed = lax.ppermute(far, axes, [(t + RUN - 1, t - 1) for t in RELAYED])
    far = pl.pallas_call(
        either,
        out_shape=jax.ShapeDtypeStruct((ROWS, 128), f32),
        in_specs=[vmem] * 3,
        out_specs=vmem,
        compiler_params=pltpu.CompilerParams(vmem_limit_bytes=2**21),
        cost_estimate=pl.CostEstimate(flops=LATE_COST, bytes_accessed=2**16, transcendentals=0),
        name="either",
    )(far, late, passed)
    return pl.pallas_call(
        gradient,
        out_shape=jax.ShapeDtypeStruct((OWN_COLS, ROWS), f32),
        in_specs=[vmem] * 4,
        out_specs=hbm,
        scratch_shapes=[
            pltpu.VMEM((CHANNELS, FLAT), f32),
            pltpu.VMEM((FLAT, 128), f32),
            pltpu.VMEM((FIELD_ROWS, FLAT), bf16),
            pltpu.VMEM((TAPS, 112, 128), bf16),
            pltpu.VMEM((TAPS, 96, 128), bf16),
            pltpu.VMEM((FIELD_ROWS * (FIELD_BLOCKS - 1), 256), bf16),
            pltpu.VMEM((GROUP * TAP_PITCH, CHANNELS * PITCH), bf16),
            pltpu.VMEM((OWN_COLS, ROWS), f32),
            pltpu.SemaphoreType.DMA,
        ],
        compiler_params=pltpu.CompilerParams(vmem_limit_bytes=VMEM),
        name="gradient",
    )(mask, goal, far, messages).T


def solution(mesh):
    tiles, partners = mesh.devices.shape
    mesh = jax.sharding.Mesh(mesh.devices.reshape(tiles // 2, 2, partners), ("pair", "core", "kern"))
    rows = P(("pair", "core"), None)
    return jax.shard_map(
        on_device,
        mesh=mesh,
        in_specs=(rows, rows, rows, P("kern", None, None, None), P("kern")),
        out_specs=P(("pair", "core"), "kern"),
        check_vma=False,
    )
```

```python
import functools

import jax
import jax.numpy as jnp
from jax import lax
from jax.experimental import pallas as pl
from jax.experimental.pallas import tpu as pltpu
from jax.sharding import PartitionSpec as P

steepness = 10.0
threshold = 0.4

TAPS = 35
HALF = 17
OWN_COLS = 32
PITCH = 48
FLAT = 1792
TAP_LANES = TAPS * PITCH
GROUP = 8
FIELD_BLOCKS = 9
FIELD_COLS = OWN_COLS + 2 * HALF
OUT_BLOCKS = 4
PARTNERS = 8
LOCAL = 6
CHANNELS = PARTNERS * LOCAL
ROWS = 64
RUN = 16
RELAYED = (32, 48)
RELAY = 11
LATE_COST = 33 * 10**8
SHARE = 8
HALF_FLAT = FLAT // 2
WIDTH = 256
FIELD_ROWS = GROUP * CHANNELS
TAP_PITCH = 40
DEPTH = 2048
VMEM = 50 * 1024 * 1024


def prepare(levels_hbm, jitter_hbm, target_hbm, kernels_hbm, weight_hbm,
            mask_ref, goal_ref, far_ref, message_ref,
            levels_ref, jitter_ref, target_ref, kernels_ref, weight_ref, near_ref, arrived):
    copies = [
        pltpu.make_async_copy(source, place, arrived.at[n])
        for n, (source, place) in enumerate([
            (levels_hbm, levels_ref),
            (jitter_hbm, jitter_ref),
            (target_hbm, target_ref),
            (kernels_hbm, kernels_ref),
            (weight_hbm, weight_ref),
        ])
    ]
    for copy in copies:
        copy.start()
    kern = lax.axis_index("kern")
    core = lax.axis_index("core")
    first_col = kern * OWN_COLS

    def columns(whole, before):
        shift = lax.rem(WIDTH + before - first_col, WIDTH)
        rolled = pltpu.roll(whole, shift, 1)[:, :128]
        col = lax.broadcasted_iota(jnp.int32, (ROWS, 128), 1) + (first_col - before)
        return jnp.where((col >= 0) & (col < WIDTH), rolled, 0.0)

    for copy in copies:
        copy.wait()
    logits = levels_ref[...].astype(jnp.float32) - 1.5 + jitter_ref[...]
    mask = (1.0 / (1.0 + jnp.exp(-logits))).astype(jnp.bfloat16).astype(jnp.float32)
    goal = target_ref[...].astype(jnp.float32)
    own_mask = columns(mask, 2 * HALF)
    own_goal = columns(goal, HALF)
    mask_ref[...] = own_mask
    goal_ref[...] = own_goal
    odd = core == 1
    far_mask = jnp.where(odd, own_mask[24:64], own_mask[0:40])
    far_goal = jnp.where(odd, own_goal[40:64], own_goal[0:24])
    far_ref[...] = jnp.concatenate([far_mask, far_goal], 0).astype(jnp.bfloat16)
    near_ref[0:40] = jnp.where(odd, mask[0:40], mask[24:64])
    near_goal = jnp.where(odd, goal[0:24], goal[40:64])
    near_ref[40:64] = pltpu.roll(near_goal, WIDTH - HALF, 1)
    share = near_ref[pl.ds(pl.multiple_of(kern * SHARE, SHARE), SHARE), :]
    lane = lax.broadcasted_iota(jnp.int32, (SHARE, 128), 1)
    shares = []
    for partner in range(PARTNERS):
        start = partner * OWN_COLS - 2 * HALF
        rolled = pltpu.roll(share, (-start) % WIDTH, 1)[:, :128]
        inside = (lane >= -start) & (lane < WIDTH - start)
        shares.append(jnp.where(inside | (kern >= 40 // SHARE), rolled, 0.0).astype(jnp.bfloat16))

    taps = kernels_ref[...].astype(jnp.float32)
    gap = jnp.zeros((LOCAL, PITCH - TAPS), jnp.float32)
    pieces = []
    for i in range(TAPS):
        pieces += [jnp.concatenate([taps[k, i] for k in range(LOCAL // 2)], 0), gap]
    row = lax.broadcasted_iota(jnp.int32, (LOCAL, 1), 0)
    weight = jnp.where(row < 2, weight_ref[0], jnp.where(row < 4, weight_ref[1], weight_ref[2]))
    high = weight.astype(jnp.bfloat16).astype(jnp.float32)
    middle = (weight - high).astype(jnp.bfloat16).astype(jnp.float32)
    low = weight - high - middle
    lane = lax.broadcasted_iota(jnp.int32, (LOCAL, FLAT - TAP_LANES), 1)
    tail = jnp.where(lane == 0, high, jnp.where(lane == 1, middle, jnp.where(lane == 2, low, 0.0)))
    flat = jnp.concatenate(pieces + [tail], 1)
    part = jnp.where(odd, flat[:, HALF_FLAT:], flat[:, :HALF_FLAT])
    part = jnp.concatenate([part, jnp.zeros((SHARE - LOCAL, HALF_FLAT), jnp.float32)], 0).astype(jnp.bfloat16)
    for partner in range(PARTNERS):
        message = jnp.concatenate([part, shares[partner]], 1)
        for to_core in range(2):
            message_ref[PARTNERS * to_core + partner] = message


def either(far_ref, late_ref, passed_ref, rows_ref):
    far = far_ref[...].astype(jnp.float32)
    rows_ref[...] = far + late_ref[...].astype(jnp.float32) + passed_ref[...].astype(jnp.float32)


def gradient(mask_ref, goal_ref, far_ref, message_ref, out_hbm,
             flat_ref, turned_ref, band_ref, even_ref, odd_ref, adjoint_ref, back_ref, out_ref, sent):
    core = lax.axis_index("core")
    tile = lax.axis_index("pair") * 2 + core
    tiles = lax.axis_size("pair") * 2
    kern = lax.axis_index("kern")
    far = far_ref[...]
    near = jnp.concatenate(
        [message_ref[(1 - core) * PARTNERS + k, :, HALF_FLAT:].astype(jnp.float32) for k in range(PARTNERS)], 0
    )
    up = jnp.where(core == 1, near, far)
    down = jnp.where(core == 1, far, near)

    line = lax.broadcasted_iota(jnp.int32, (16, 128), 0) + 88
    mask = mask_ref[...]

    def circle(first_up):
        mixed = jnp.where(line >= first_up, up[0:16], down[24:40])
        return jnp.concatenate([mask, down[0:24], mixed, up[16:40]], 0).T

    image_above = circle(94)
    image_below = circle(98)
    goal = jnp.concatenate(
        [goal_ref[...], down[40:64], jnp.zeros((16, 128), jnp.float32), up[40:64]], 0
    ).T

    for i in range(TAPS):
        source = image_above if i < HALF else image_below
        turned = pltpu.roll(source, (HALF - i) % 128, 1)
        even_ref[i] = turned[0:112].astype(jnp.bfloat16)
        odd_ref[i] = turned[8:104].astype(jnp.bfloat16)

    for partner in range(PARTNERS):
        for half in range(2):
            part = message_ref[PARTNERS * half + partner, :, :HALF_FLAT].astype(jnp.float32)
            flat_ref[LOCAL * partner : LOCAL * (partner + 1), HALF_FLAT * half : HALF_FLAT * (half + 1)] = part[:LOCAL]
    last = flat_ref[:, TAP_LANES : TAP_LANES + 3]
    weight = last[:, 0:1] + last[:, 1:2] + last[:, 2:3]
    lane = lax.broadcasted_iota(jnp.int32, (CHANNELS, FLAT), 1)
    flat = jnp.where(lane < TAP_LANES, flat_ref[...], 0.0)
    for d in range(GROUP):
        shifted = flat if d == 0 else pltpu.roll(flat, d, 1)
        band_ref[CHANNELS * d : CHANNELS * (d + 1), :] = shifted.astype(jnp.bfloat16)

    turned_ref[...] = jnp.concatenate([flat, jnp.zeros((128 - CHANNELS, FLAT), jnp.float32)], 0).T
    pieces = []
    for j in range(TAPS):
        pieces.append(turned_ref[pl.ds(TAPS - 1 - j, TAPS, stride=PITCH), :][:, :CHANNELS])
    pieces.append(jnp.zeros((TAPS, CHANNELS * (PITCH - TAPS)), jnp.float32))
    backward = jnp.concatenate(pieces, 1)
    backward = jnp.concatenate(
        [backward, jnp.zeros((TAP_PITCH - TAPS, CHANNELS * PITCH), jnp.float32)], 0
    )
    for d in range(GROUP):
        shifted = backward if d == 0 else pltpu.roll(backward, CHANNELS * d, 1)
        back_ref[TAP_PITCH * d : TAP_PITCH * (d + 1), :] = shifted.astype(jnp.bfloat16)

    at = lax.broadcasted_iota(jnp.int32, (GROUP, 128), 1)
    at = jnp.where(at < 96, at, at - 128)
    row_in_clip = at + tile * ROWS
    row_ok = (row_in_clip >= 0) & (row_in_clip < tiles * ROWS)
    step = lax.broadcasted_iota(jnp.int32, (GROUP, 128), 0)
    for first in range(0, FIELD_BLOCKS, 2):
        count = min(2, FIELD_BLOCKS - first)
        groups = min(GROUP, FIELD_COLS - GROUP * first)
        together = jnp.dot(
            band_ref[: CHANNELS * groups, :TAP_LANES],
            jnp.concatenate([
                (even_ref if b % 2 == 0 else odd_ref)[:, 16 * (b // 2) : 16 * (b // 2) + PITCH, :].reshape(TAP_LANES, 128)
                for b in range(first, first + count)
            ], 1),
            preferred_element_type=jnp.float32,
        )
        for b in range(first, first + count):
            fields = together[:, 128 * (b - first) : 128 * (b - first + 1)]
            fields = fields.reshape(groups, CHANNELS, 128)
            weighted = fields * weight[None]
            intensity = jnp.sum(weighted * fields, axis=1)
            resist = 1.0 / (1.0 + jnp.exp(-steepness * (intensity - threshold)))
            drive = 2.0 * (resist - goal[8 * b : 8 * b + groups]) * steepness * resist * (1.0 - resist)
            col = step[:groups] + (8 * b - HALF + kern * OWN_COLS)
            drive = jnp.where(row_ok[:groups] & (col >= 0) & (col < WIDTH), drive, 0.0)
            adjoint = (2.0 * weighted * drive[:, None, :]).astype(jnp.bfloat16).reshape(CHANNELS * groups, 128)
            if groups < GROUP:
                rest = jnp.zeros((FIELD_ROWS - CHANNELS * groups, 128), jnp.bfloat16)
                adjoint = jnp.concatenate([adjoint, rest], 0)
            if b < FIELD_BLOCKS - 1:
                adjoint_ref[FIELD_ROWS * b : FIELD_ROWS * (b + 1), 0:128] = adjoint
            if b > 0:
                adjoint_ref[FIELD_ROWS * (b - 1) : FIELD_ROWS * b, 128:256] = adjoint

    grads = []
    for n in range(OUT_BLOCKS // 2):
        spread = jnp.dot(
            back_ref[:, :DEPTH],
            adjoint_ref[2 * FIELD_ROWS * n : 2 * FIELD_ROWS * n + DEPTH, :],
            preferred_element_type=jnp.float32,
        )
        for half in range(2):
            for d in range(GROUP):
                part = spread[TAP_PITCH * d : TAP_PITCH * (d + 1), 128 * half : 128 * (half + 1)]
                part = pltpu.roll(part, 0, 1, stride=1, stride_axis=0)
                grads.append(jnp.sum(part, axis=0, keepdims=True))
    out_ref[...] = pltpu.roll(jnp.concatenate(grads, 0), 128 - HALF, 1)[:, :ROWS]
    copy = pltpu.make_async_copy(out_ref, out_hbm, sent)
    copy.start()
    copy.wait()


def on_device(levels, jitter, target, kernels, kernel_weight):
    vmem = pl.BlockSpec(memory_space=pltpu.VMEM)
    hbm = pl.BlockSpec(memory_space=pltpu.HBM)
    f32, bf16 = jnp.float32, jnp.bfloat16
    mask, goal, to_far, message = pl.pallas_call(
        prepare,
        out_shape=(
            jax.ShapeDtypeStruct((ROWS, 128), f32),
            jax.ShapeDtypeStruct((ROWS, 128), f32),
            jax.ShapeDtypeStruct((ROWS, 128), bf16),
            jax.ShapeDtypeStruct((2 * PARTNERS, SHARE, HALF_FLAT + 128), bf16),
        ),
        in_specs=[hbm] * 5,
        out_specs=(vmem,) * 4,
        scratch_shapes=[
            pltpu.VMEM((ROWS, WIDTH), jnp.int32),
            pltpu.VMEM((ROWS, WIDTH), f32),
            pltpu.VMEM((ROWS, WIDTH), jnp.int32),
            pltpu.VMEM((LOCAL // 2, TAPS, 2, TAPS), bf16),
            pltpu.SMEM((LOCAL // 2,), f32),
            pltpu.VMEM((ROWS, WIDTH), f32),
            pltpu.SemaphoreType.DMA((5,)),
        ],
        compiler_params=pltpu.CompilerParams(vmem_limit_bytes=VMEM),
        name="prepare",
    )(*(
        pltpu.with_memory_space_constraint(x, pltpu.HBM)
        for x in (levels, jitter, target, kernels.transpose(0, 2, 1, 3), kernel_weight)
    ))
    tiles = lax.axis_size("pair") * 2
    axes = ("pair", "core")
    starts = range(RUN, tiles, RUN)
    late = lax.ppermute(to_far, axes, [(t - 1, t) for t in starts])
    messages = lax.all_to_all(message, ("core", "kern"), 0, 0)
    meet = [(t, t + 1) for t in range(1, tiles - 1, 2)]
    moves = [(a, b) for a, b in meet if b not in starts]
    moves += [(b, a) for a, b in meet if b not in RELAYED]
    ends = lax.axis_index(axes) % RUN == RUN - 1
    relayed = lax.ppermute(jnp.where(ends, late, to_far), axes, [(t, t + RELAY) for t in RELAYED])
    far = lax.ppermute(to_far, axes, moves)
    passed = lax.ppermute(relayed, axes, [(t + RELAY, t - 1) for t in RELAYED])
    far = pl.pallas_call(
        either,
        out_shape=jax.ShapeDtypeStruct((ROWS, 128), f32),
        in_specs=[vmem] * 3,
        out_specs=vmem,
        compiler_params=pltpu.CompilerParams(vmem_limit_bytes=2**21),
        cost_estimate=pl.CostEstimate(flops=LATE_COST, bytes_accessed=2**16, transcendentals=0),
        name="either",
    )(far, late, passed)
    return pl.pallas_call(
        gradient,
        out_shape=jax.ShapeDtypeStruct((OWN_COLS, ROWS), f32),
        in_specs=[vmem] * 4,
        out_specs=hbm,
        scratch_shapes=[
            pltpu.VMEM((CHANNELS, FLAT), f32),
            pltpu.VMEM((FLAT, 128), f32),
            pltpu.VMEM((FIELD_ROWS, FLAT), bf16),
            pltpu.VMEM((TAPS, 112, 128), bf16),
            pltpu.VMEM((TAPS, 96, 128), bf16),
            pltpu.VMEM((FIELD_ROWS * (FIELD_BLOCKS - 1), 256), bf16),
            pltpu.VMEM((GROUP * TAP_PITCH, CHANNELS * PITCH), bf16),
            pltpu.VMEM((OWN_COLS, ROWS), f32),
            pltpu.SemaphoreType.DMA,
        ],
        compiler_params=pltpu.CompilerParams(vmem_limit_bytes=VMEM),
        name="gradient",
    )(mask, goal, far, messages).T


def solution(mesh):
    tiles, partners = mesh.devices.shape
    mesh = jax.sharding.Mesh(mesh.devices.reshape(tiles // 2, 2, partners), ("pair", "core", "kern"))
    rows = P(("pair", "core"), None)
    return jax.shard_map(
        on_device,
        mesh=mesh,
        in_specs=(rows, rows, rows, P("kern", None, None, None), P("kern")),
        out_specs=P(("pair", "core"), "kern"),
        check_vma=False,
    )
```

```python
import functools

import jax
import jax.numpy as jnp
from jax import lax
from jax.experimental import pallas as pl
from jax.experimental.pallas import tpu as pltpu
from jax.sharding import PartitionSpec as P

steepness = 10.0
threshold = 0.4

TAPS = 35
HALF = 17
OWN_COLS = 32
PITCH = 48
FLAT = 1792
TAP_LANES = TAPS * PITCH
GROUP = 8
FIELD_BLOCKS = 9
FIELD_COLS = OWN_COLS + 2 * HALF
OUT_BLOCKS = 4
PARTNERS = 8
LOCAL = 6
CHANNELS = PARTNERS * LOCAL
ROWS = 64
RUN = 16
RELAYED = (32, 48)
LATE_COST = 33 * 10**8
SHARE = 8
HALF_FLAT = FLAT // 2
WIDTH = 256
FIELD_ROWS = GROUP * CHANNELS
TAP_PITCH = 40
DEPTH = 2048
VMEM = 50 * 1024 * 1024


def prepare(levels_hbm, jitter_hbm, target_hbm, kernels_hbm, weight_hbm,
            mask_ref, goal_ref, far_ref, message_ref,
            levels_ref, jitter_ref, target_ref, kernels_ref, weight_ref, near_ref, arrived):
    copies = [
        pltpu.make_async_copy(source, place, arrived.at[n])
        for n, (source, place) in enumerate([
            (levels_hbm, levels_ref),
            (jitter_hbm, jitter_ref),
            (target_hbm, target_ref),
            (kernels_hbm, kernels_ref),
            (weight_hbm, weight_ref),
        ])
    ]
    for copy in copies:
        copy.start()
    kern = lax.axis_index("kern")
    core = lax.axis_index("core")
    first_col = kern * OWN_COLS

    def columns(whole, before):
        shift = lax.rem(WIDTH + before - first_col, WIDTH)
        rolled = pltpu.roll(whole, shift, 1)[:, :128]
        col = lax.broadcasted_iota(jnp.int32, (ROWS, 128), 1) + (first_col - before)
        return jnp.where((col >= 0) & (col < WIDTH), rolled, 0.0)

    for copy in copies:
        copy.wait()
    logits = levels_ref[...].astype(jnp.float32) - 1.5 + jitter_ref[...]
    mask = (1.0 / (1.0 + jnp.exp(-logits))).astype(jnp.bfloat16).astype(jnp.float32)
    goal = target_ref[...].astype(jnp.float32)
    own_mask = columns(mask, 2 * HALF)
    own_goal = columns(goal, HALF)
    mask_ref[...] = own_mask
    goal_ref[...] = own_goal
    odd = core == 1
    far_mask = jnp.where(odd, own_mask[24:64], own_mask[0:40])
    far_goal = jnp.where(odd, own_goal[40:64], own_goal[0:24])
    far_ref[...] = jnp.concatenate([far_mask, far_goal], 0).astype(jnp.bfloat16)
    near_ref[0:40] = jnp.where(odd, mask[0:40], mask[24:64])
    near_goal = jnp.where(odd, goal[0:24], goal[40:64])
    near_ref[40:64] = pltpu.roll(near_goal, WIDTH - HALF, 1)
    share = near_ref[pl.ds(pl.multiple_of(kern * SHARE, SHARE), SHARE), :]
    lane = lax.broadcasted_iota(jnp.int32, (SHARE, 128), 1)
    shares = []
    for partner in range(PARTNERS):
        start = partner * OWN_COLS - 2 * HALF
        rolled = pltpu.roll(share, (-start) % WIDTH, 1)[:, :128]
        inside = (lane >= -start) & (lane < WIDTH - start)
        shares.append(jnp.where(inside | (kern >= 40 // SHARE), rolled, 0.0).astype(jnp.bfloat16))

    taps = kernels_ref[...].astype(jnp.float32)
    gap = jnp.zeros((LOCAL, PITCH - TAPS), jnp.float32)
    pieces = []
    for i in range(TAPS):
        pieces += [jnp.concatenate([taps[k, i] for k in range(LOCAL // 2)], 0), gap]
    row = lax.broadcasted_iota(jnp.int32, (LOCAL, 1), 0)
    weight = jnp.where(row < 2, weight_ref[0], jnp.where(row < 4, weight_ref[1], weight_ref[2]))
    high = weight.astype(jnp.bfloat16).astype(jnp.float32)
    middle = (weight - high).astype(jnp.bfloat16).astype(jnp.float32)
    low = weight - high - middle
    lane = lax.broadcasted_iota(jnp.int32, (LOCAL, FLAT - TAP_LANES), 1)
    tail = jnp.where(lane == 0, high, jnp.where(lane == 1, middle, jnp.where(lane == 2, low, 0.0)))
    flat = jnp.concatenate(pieces + [tail], 1)
    part = jnp.where(odd, flat[:, HALF_FLAT:], flat[:, :HALF_FLAT])
    part = jnp.concatenate([part, jnp.zeros((SHARE - LOCAL, HALF_FLAT), jnp.float32)], 0).astype(jnp.bfloat16)
    for partner in range(PARTNERS):
        message = jnp.concatenate([part, shares[partner]], 1)
        for to_core in range(2):
            message_ref[PARTNERS * to_core + partner] = message


def either(far_ref, late_ref, passed_ref, rows_ref):
    tile = lax.axis_index("pair") * 2 + lax.axis_index("core")
    far = far_ref[...].astype(jnp.float32)
    for start in RELAYED:
        far = jnp.where(tile == start + RUN - 1, 0.0, far)
    rows_ref[...] = far + late_ref[...].astype(jnp.float32) + passed_ref[...].astype(jnp.float32)


def gradient(mask_ref, goal_ref, far_ref, message_ref, out_hbm,
             flat_ref, turned_ref, band_ref, even_ref, odd_ref, adjoint_ref, back_ref, out_ref, sent):
    core = lax.axis_index("core")
    tile = lax.axis_index("pair") * 2 + core
    tiles = lax.axis_size("pair") * 2
    kern = lax.axis_index("kern")
    far = far_ref[...]
    near = jnp.concatenate(
        [message_ref[(1 - core) * PARTNERS + k, :, HALF_FLAT:].astype(jnp.float32) for k in range(PARTNERS)], 0
    )
    up = jnp.where(core == 1, near, far)
    down = jnp.where(core == 1, far, near)

    line = lax.broadcasted_iota(jnp.int32, (16, 128), 0) + 88
    mask = mask_ref[...]

    def circle(first_up):
        mixed = jnp.where(line >= first_up, up[0:16], down[24:40])
        return jnp.concatenate([mask, down[0:24], mixed, up[16:40]], 0).T

    image_above = circle(94)
    image_below = circle(98)
    goal = jnp.concatenate(
        [goal_ref[...], down[40:64], jnp.zeros((16, 128), jnp.float32), up[40:64]], 0
    ).T

    for i in range(TAPS):
        source = image_above if i < HALF else image_below
        turned = pltpu.roll(source, (HALF - i) % 128, 1)
        even_ref[i] = turned[0:112].astype(jnp.bfloat16)
        odd_ref[i] = turned[8:104].astype(jnp.bfloat16)

    for partner in range(PARTNERS):
        for half in range(2):
            part = message_ref[PARTNERS * half + partner, :, :HALF_FLAT].astype(jnp.float32)
            flat_ref[LOCAL * partner : LOCAL * (partner + 1), HALF_FLAT * half : HALF_FLAT * (half + 1)] = part[:LOCAL]
    last = flat_ref[:, TAP_LANES : TAP_LANES + 3]
    weight = last[:, 0:1] + last[:, 1:2] + last[:, 2:3]
    lane = lax.broadcasted_iota(jnp.int32, (CHANNELS, FLAT), 1)
    flat = jnp.where(lane < TAP_LANES, flat_ref[...], 0.0)
    for d in range(GROUP):
        shifted = flat if d == 0 else pltpu.roll(flat, d, 1)
        band_ref[CHANNELS * d : CHANNELS * (d + 1), :] = shifted.astype(jnp.bfloat16)

    turned_ref[...] = jnp.concatenate([flat, jnp.zeros((128 - CHANNELS, FLAT), jnp.float32)], 0).T
    pieces = []
    for j in range(TAPS):
        pieces.append(turned_ref[pl.ds(TAPS - 1 - j, TAPS, stride=PITCH), :][:, :CHANNELS])
    pieces.append(jnp.zeros((TAPS, CHANNELS * (PITCH - TAPS)), jnp.float32))
    backward = jnp.concatenate(pieces, 1)
    backward = jnp.concatenate(
        [backward, jnp.zeros((TAP_PITCH - TAPS, CHANNELS * PITCH), jnp.float32)], 0
    )
    for d in range(GROUP):
        shifted = backward if d == 0 else pltpu.roll(backward, CHANNELS * d, 1)
        back_ref[TAP_PITCH * d : TAP_PITCH * (d + 1), :] = shifted.astype(jnp.bfloat16)

    at = lax.broadcasted_iota(jnp.int32, (GROUP, 128), 1)
    at = jnp.where(at < 96, at, at - 128)
    row_in_clip = at + tile * ROWS
    row_ok = (row_in_clip >= 0) & (row_in_clip < tiles * ROWS)
    step = lax.broadcasted_iota(jnp.int32, (GROUP, 128), 0)
    for first in (FIELD_BLOCKS - 1, *range(0, FIELD_BLOCKS - 1, 2)):
        count = min(2, FIELD_BLOCKS - first)
        groups = min(GROUP, FIELD_COLS - GROUP * first)
        together = jnp.dot(
            band_ref[: CHANNELS * groups, :TAP_LANES],
            jnp.concatenate([
                (even_ref if b % 2 == 0 else odd_ref)[:, 16 * (b // 2) : 16 * (b // 2) + PITCH, :].reshape(TAP_LANES, 128)
                for b in range(first, first + count)
            ], 1),
            preferred_element_type=jnp.float32,
        )
        for b in range(first, first + count):
            fields = together[:, 128 * (b - first) : 128 * (b - first + 1)]
            fields = fields.reshape(groups, CHANNELS, 128)
            weighted = fields * weight[None]
            intensity = jnp.sum(weighted * fields, axis=1)
            resist = 1.0 / (1.0 + jnp.exp(-steepness * (intensity - threshold)))
            drive = 2.0 * (resist - goal[8 * b : 8 * b + groups]) * steepness * resist * (1.0 - resist)
            col = step[:groups] + (8 * b - HALF + kern * OWN_COLS)
            drive = jnp.where(row_ok[:groups] & (col >= 0) & (col < WIDTH), drive, 0.0)
            adjoint = (2.0 * weighted * drive[:, None, :]).astype(jnp.bfloat16).reshape(CHANNELS * groups, 128)
            if groups < GROUP:
                rest = jnp.zeros((FIELD_ROWS - CHANNELS * groups, 128), jnp.bfloat16)
                adjoint = jnp.concatenate([adjoint, rest], 0)
            if b < FIELD_BLOCKS - 1:
                adjoint_ref[FIELD_ROWS * b : FIELD_ROWS * (b + 1), 0:128] = adjoint
            if b > 0:
                adjoint_ref[FIELD_ROWS * (b - 1) : FIELD_ROWS * b, 128:256] = adjoint

    grads = []
    for n in range(OUT_BLOCKS // 2):
        spread = jnp.dot(
            back_ref[:, :DEPTH],
            adjoint_ref[2 * FIELD_ROWS * n : 2 * FIELD_ROWS * n + DEPTH, :],
            preferred_element_type=jnp.float32,
        )
        for half in range(2):
            for d in range(GROUP):
                part = spread[TAP_PITCH * d : TAP_PITCH * (d + 1), 128 * half : 128 * (half + 1)]
                part = pltpu.roll(part, 0, 1, stride=1, stride_axis=0)
                grads.append(jnp.sum(part, axis=0, keepdims=True))
    out_ref[...] = pltpu.roll(jnp.concatenate(grads, 0), 128 - HALF, 1)[:, :ROWS]
    copy = pltpu.make_async_copy(out_ref, out_hbm, sent)
    copy.start()
    copy.wait()


def on_device(levels, jitter, target, kernels, kernel_weight):
    vmem = pl.BlockSpec(memory_space=pltpu.VMEM)
    hbm = pl.BlockSpec(memory_space=pltpu.HBM)
    f32, bf16 = jnp.float32, jnp.bfloat16
    mask, goal, to_far, message = pl.pallas_call(
        prepare,
        out_shape=(
            jax.ShapeDtypeStruct((ROWS, 128), f32),
            jax.ShapeDtypeStruct((ROWS, 128), f32),
            jax.ShapeDtypeStruct((ROWS, 128), bf16),
            jax.ShapeDtypeStruct((2 * PARTNERS, SHARE, HALF_FLAT + 128), bf16),
        ),
        in_specs=[hbm] * 5,
        out_specs=(vmem,) * 4,
        scratch_shapes=[
            pltpu.VMEM((ROWS, WIDTH), jnp.int32),
            pltpu.VMEM((ROWS, WIDTH), f32),
            pltpu.VMEM((ROWS, WIDTH), jnp.int32),
            pltpu.VMEM((LOCAL // 2, TAPS, 2, TAPS), bf16),
            pltpu.SMEM((LOCAL // 2,), f32),
            pltpu.VMEM((ROWS, WIDTH), f32),
            pltpu.SemaphoreType.DMA((5,)),
        ],
        compiler_params=pltpu.CompilerParams(vmem_limit_bytes=VMEM),
        name="prepare",
    )(*(
        pltpu.with_memory_space_constraint(x, pltpu.HBM)
        for x in (levels, jitter, target, kernels.transpose(0, 2, 1, 3), kernel_weight)
    ))
    tiles = lax.axis_size("pair") * 2
    axes = ("pair", "core")
    starts = range(RUN, tiles, RUN)
    late = lax.ppermute(to_far, axes, [(t - 1, t) for t in starts])
    messages = lax.all_to_all(message, ("core", "kern"), 0, 0)
    meet = [(t, t + 1) for t in range(1, tiles - 1, 2)]
    moves = [(a, b) for a, b in meet if b not in starts]
    moves += [(b, a) for a, b in meet if b not in RELAYED] + [(t, t + RUN - 1) for t in RELAYED]
    ends = lax.axis_index(axes) % RUN == RUN - 1
    far = lax.ppermute(jnp.where(ends, late, to_far), axes, moves)
    passed = lax.ppermute(far, axes, [(t + RUN - 1, t - 1) for t in RELAYED])
    far = pl.pallas_call(
        either,
        out_shape=jax.ShapeDtypeStruct((ROWS, 128), f32),
        in_specs=[vmem] * 3,
        out_specs=vmem,
        compiler_params=pltpu.CompilerParams(vmem_limit_bytes=2**21),
        cost_estimate=pl.CostEstimate(flops=LATE_COST, bytes_accessed=2**16, transcendentals=0),
        name="either",
    )(far, late, passed)
    return pl.pallas_call(
        gradient,
        out_shape=jax.ShapeDtypeStruct((OWN_COLS, ROWS), f32),
        in_specs=[vmem] * 4,
        out_specs=hbm,
        scratch_shapes=[
            pltpu.VMEM((CHANNELS, FLAT), f32),
            pltpu.VMEM((FLAT, 128), f32),
            pltpu.VMEM((FIELD_ROWS, FLAT), bf16),
            pltpu.VMEM((TAPS, 112, 128), bf16),
            pltpu.VMEM((TAPS, 96, 128), bf16),
            pltpu.VMEM((FIELD_ROWS * (FIELD_BLOCKS - 1), 256), bf16),
            pltpu.VMEM((GROUP * TAP_PITCH, CHANNELS * PITCH), bf16),
            pltpu.VMEM((OWN_COLS, ROWS), f32),
            pltpu.SemaphoreType.DMA,
        ],
        compiler_params=pltpu.CompilerParams(vmem_limit_bytes=VMEM),
        name="gradient",
    )(mask, goal, far, messages).T


def solution(mesh):
    tiles, partners = mesh.devices.shape
    mesh = jax.sharding.Mesh(mesh.devices.reshape(tiles // 2, 2, partners), ("pair", "core", "kern"))
    rows = P(("pair", "core"), None)
    return jax.shard_map(
        on_device,
        mesh=mesh,
        in_specs=(rows, rows, rows, P("kern", None, None, None), P("kern")),
        out_specs=P(("pair", "core"), "kern"),
        check_vma=False,
    )
```
